128 devices in a mesh: pat: 32 (over y, z_hi, x), feat: 2 (over core), tm: 2 (over z_lo).
Axes of the slice: x: 4, y: 4, z: 4 (z_hi: 2, z_lo: 2; z = z_hi * 2 + z_lo), core: 2. Of those that a mesh axis runs over, the one named last changes fastest.
Arguments:
- tensor: float32 [256, 16, 131072], P('feat', 'tm', 'pat'), may hold values from -200 to 200
- feat_init: float32 [32, 256], P(None, 'feat'), may hold values from -6 to 6
- time_init: float32 [32, 16], P(None, 'tm'), may hold values from -6 to 6
Outputs:
- factor_pat: float32 [32, 131072], P(None, 'pat')
- factor_feat: float32 [32, 256], P(None, 'feat')
- factor_time: float32 [32, 16], P(None, 'tm')
The draws below stay inside these ranges and needn't reach their ends.
All inputs are finite; a program needn't handle non-finite values.
Results may differ from the reference program's by a relative error of at most 0.000075.
Values sent between devices are 32-bit elements; how exact they have to be, the bound alone decides.
No kernel may reach another device: no remote copies, remote signals or barrier semaphores. Data moves between devices by JAX's collectives and lax.ppermute only.
A program may use at most 64 MiB of HBM per device.

```python
import math
import jax
import jax.numpy as jnp
from jax import lax

R = 32
J = 256
K = 16
I = 131072


def draw_tensor(key, part):
    key = jax.random.fold_in(key, 7)
    subkeys = jax.random.split(key, 4)
    noise = jnp.clip(jax.random.normal(subkeys[0], (J, K, I), jnp.float32), -6.0, 6.0)
    row_scale = 10.0 ** (0.5 * jnp.arange(I, dtype=jnp.float32) / I + 0.5 * jax.random.uniform(subkeys[1], (I,), jnp.float32))
    col_scale = 10.0 ** (0.5 * jnp.arange(J, dtype=jnp.float32) / J + 0.5 * jax.random.uniform(subkeys[2], (J,), jnp.float32))
    time_scale = 10.0 ** (0.5 * jax.random.uniform(subkeys[3], (K,), jnp.float32))
    return noise * col_scale[:, None, None] * time_scale[None, :, None] * row_scale[None, None, :] * 0.1


def block_scale(own_key, extent, cuts, low, high):
    level = 1.0
    for dim, parts in cuts:
        steps = jax.random.uniform(jax.random.fold_in(jax.random.fold_in(own_key, 6), dim), (parts,), jnp.float32, low / len(cuts), high / len(cuts))
        level = level * jnp.repeat(jnp.exp(steps), extent[dim] // parts).reshape((-1,) + (1,) * (len(extent) - 1 - dim))
    return level


def scatter_about(rng, dims, spread, bound, cuts=(), kind=jnp.bfloat16):
    values = jax.random.normal(rng, dims, jnp.float32) * spread
    if len(cuts) > 0:
        values = block_scale(rng, dims, cuts, -0.22, 0.18) * values
    return jnp.clip(values, min=-bound, max=bound).astype(kind)


def setup_inputs(seed: int = 0) -> dict:
    key_of = jax.random.split(jax.random.key(seed), 4)
    tensor = draw_tensor(jax.random.fold_in(key_of[3], 71), 0)
    feat_init = scatter_about(key_of[1], (R, J), 1.0, 6.0, ((1, 2),), jnp.float32)
    time_init = scatter_about(key_of[2], (R, K), 1.0, 6.0, ((1, 2),), jnp.float32)
    return dict(tensor=tensor, feat_init=feat_init, time_init=time_init)


highest = lax.Precision.HIGHEST
epsilon = 1e-06

def gram_of(factor):
    return jnp.dot(factor, factor.T, precision=highest)

def solve_system(system, terms):
    lower = jnp.linalg.cholesky(system)
    return jax.scipy.linalg.cho_solve((lower, True), terms)

def scale_rows(raw_factor):
    mean_square = lax.optimization_barrier(jnp.mean(raw_factor * raw_factor, axis=1, keepdims=True))
    return raw_factor / jnp.sqrt(mean_square + epsilon)

def reference(tensor, feat_init, time_init):
    flat = tensor.reshape(J * K, I)
    khatri_rao = (feat_init[:, :, None] * time_init[:, None, :]).reshape(R, J * K)
    pat_terms = jnp.dot(khatri_rao, flat, precision=highest)
    time_gram0 = gram_of(time_init)
    pat_raw = solve_system(gram_of(feat_init) * time_gram0, pat_terms)
    factor_pat = scale_rows(pat_raw)
    pat_gram = gram_of(factor_pat) / I
    weighted = lax.dot_general(factor_pat, flat, (((1,), (1,)), ((), ())), precision=highest).reshape(R, J, K)
    feat_terms = lax.optimization_barrier(jnp.sum(weighted * time_init[:, None, :], axis=2))
    feat_raw = solve_system(pat_gram * time_gram0, feat_terms)
    factor_feat = scale_rows(feat_raw)
    feat_gram = gram_of(factor_feat) / J
    time_terms = lax.optimization_barrier(jnp.sum(weighted * factor_feat[:, :, None], axis=1))
    factor_time = solve_system(pat_gram * feat_gram, time_terms) * (1.0 / math.sqrt(I * J))
    return (factor_pat, factor_feat, factor_time)
```

```python
import math

import jax
import jax.numpy as jnp
from jax import lax
from jax.experimental import pallas as pl
from jax.experimental.pallas import tpu as pltpu
from jax.sharding import PartitionSpec as P

f32, bf16 = jnp.float32, jnp.bfloat16
highest = lax.Precision.HIGHEST
epsilon = 1e-06
VMEM = pl.BlockSpec(memory_space=pltpu.VMEM)
HBM = pl.BlockSpec(memory_space=pltpu.HBM)
NN = (((1,), (0,)), ((), ()))
NT = (((1,), (1,)), ((), ()))
LANES = 128


def exact(a, b, dims=NN):
    return lax.dot_general(a, b, dims, precision=highest, preferred_element_type=f32)


def quick(a, b, dims=NN):
    return lax.dot_general(a, b, dims, preferred_element_type=f32)


def split(x):
    hi = x.astype(bf16)
    return hi, (x - hi.astype(f32)).astype(bf16)


def iota(shape, dim):
    return lax.broadcasted_iota(jnp.int32, shape, dim)


def one_hot_feat(feat, time):
    shape = (feat, feat * time)
    return jnp.where(lax.div(iota(shape, 1), time) == iota(shape, 0), 1.0, 0.0).astype(f32)


def one_hot_time(feat, time):
    shape = (time, feat * time)
    return jnp.where(lax.rem(iota(shape, 1), time) == iota(shape, 0), 1.0, 0.0).astype(f32)


def eliminate(tiles, group=8):
    rank = tiles[0].shape[0]
    rows = iota((rank, LANES), 0)
    for start in range(0, rank, group):
        columns = [
            jnp.broadcast_to(tiles[0][:, start + t : start + t + 1], (rank, LANES)) for t in range(group)
        ]
        for t in range(group):
            at = start + t
            column = columns[t]
            inverse = 1.0 / column[at : at + 1, :]
            here = rows == at
            for later in range(t + 1, group):
                scaled = columns[later][at : at + 1, :] * inverse
                columns[later] = jnp.where(here, scaled, columns[later] - column * scaled)
            new = []
            for tile in tiles:
                scaled = tile[at : at + 1, :] * inverse
                new.append(jnp.where(here, scaled, tile - column * scaled))
            tiles = new
    return tiles


def wide(x, columns=LANES):
    return jnp.concatenate([x, jnp.zeros((x.shape[0], columns - x.shape[1]), f32)], axis=1)


def call(body, out_shape, name, specs, scratch=(), limit=24, flops=0, moved=0):
    return pl.pallas_call(
        body,
        out_shape=[jax.ShapeDtypeStruct(s, d) for s, d in out_shape],
        in_specs=specs,
        out_specs=[VMEM] * len(out_shape),
        scratch_shapes=list(scratch),
        compiler_params=pltpu.CompilerParams(vmem_limit_bytes=limit * 2**20),
        cost_estimate=pl.CostEstimate(flops=flops, bytes_accessed=moved, transcendentals=0),
        name=name,
    )


CHUNK = 256
DEPTH = 256


def terms_of_half(hl_ref, block_ref, kept_ref, terms_ref, sems, first, build=None):
    rank = terms_ref.shape[0]
    cells, half = kept_ref.shape
    copies = []
    for c in range(half // CHUNK):
        start = pl.multiple_of(first + c * CHUNK, CHUNK)
        copies.append(
            pltpu.make_async_copy(
                block_ref.at[:, pl.ds(start, CHUNK)], kept_ref.at[:, pl.ds(c * CHUNK, CHUNK)], sems.at[c]
            )
        )
    for copy in copies:
        copy.start()
    if build is not None:
        build()
    for c, copy in enumerate(copies):
        copy.wait()
        total = None
        for d in range(0, cells, DEPTH):
            hi, lo = split(kept_ref[d : d + DEPTH, c * CHUNK : (c + 1) * CHUNK])
            both = quick(hl_ref[:, d : d + DEPTH], hi)
            part = both[:rank] + both[rank:] + quick(hl_ref[:rank, d : d + DEPTH], lo)
            total = part if total is None else total + part
        terms_ref[:, c * CHUNK : (c + 1) * CHUNK] = total


def first_half(feat_ref, time_ref, block_ref, terms_ref, kept_ref, hl_ref, sems):
    half = kept_ref.shape[1]

    def build():
        feat, time = feat_ref[...], time_ref[...]
        count = (feat.shape[1], time.shape[1])
        product = exact(feat, one_hot_feat(*count)) * exact(time, one_hot_time(*count))
        hi, lo = split(product)
        hl_ref[...] = jnp.concatenate([hi, lo], axis=0)

    other = 1 - lax.axis_index("feat")
    terms_of_half(hl_ref, block_ref, kept_ref, terms_ref, sems, other * half, build)


def second_half(hl_ref, block_ref, terms_ref, kept_ref, sems):
    half = kept_ref.shape[1]
    terms_of_half(hl_ref, block_ref, kept_ref, terms_ref, sems, lax.axis_index("feat") * half)


def start_system(feat_ref, feat_other_ref, time_ref, time_other_ref, inverse_ref, time_gram_ref):
    rank = feat_ref.shape[0]
    feat, feat_other = feat_ref[...], feat_other_ref[...]
    time, time_other = time_ref[...], time_other_ref[...]
    time_gram = exact(time, time, NT) + exact(time_other, time_other, NT)
    system = (exact(feat, feat, NT) + exact(feat_other, feat_other, NT)) * time_gram
    eye = jnp.where(iota((rank, rank), 0) == iota((rank, rank), 1), 1.0, 0.0).astype(f32)
    (solved,) = eliminate([wide(jnp.concatenate([system, eye], axis=1))])
    inverse_ref[...] = solved[:, rank : 2 * rank]
    time_gram_ref[...] = time_gram


def solve_pat(inverse_ref, *refs):
    ins, (out_ref,) = refs[:-1], refs[-1:]
    pairs = len(ins) // 2
    width = out_ref.shape[1] // pairs
    for i in range(pairs):
        out_ref[:, i * width : (i + 1) * width] = exact(inverse_ref[...], ins[i][...] + ins[pairs + i][...])


def weigh(raw_ref, kept_ref, *refs):
    before, out_ref = (refs[0], refs[1]) if len(refs) == 2 else (None, refs[0])
    rank, half = raw_ref.shape
    cells = kept_ref.shape[0]
    hi, lo = split(raw_ref[...])
    hl = jnp.concatenate([hi, lo], axis=0)
    total = None
    for c in range(0, half, 512):
        kept_hi, kept_lo = split(kept_ref[:, c : c + 512])
        both = quick(kept_hi, hl[:, c : c + 512], NT)
        part = both[:, :rank] + both[:, rank:] + quick(kept_lo, hl[:rank, c : c + 512], NT)
        total = part if total is None else total + part
    weighted = total.T
    gram = wide(exact(raw_ref[...], raw_ref[...], NT))
    if before is not None:
        weighted = weighted + before[:, :cells]
        gram = gram + before[:, cells:]
    out_ref[:, :cells] = weighted
    out_ref[:, cells:] = gram


def add_four(a_ref, b_ref, c_ref, d_ref, out_ref):
    out_ref[...] = (a_ref[...] + b_ref[...]) + (c_ref[...] + d_ref[...])


def add_and_project(a_ref, b_ref, c_ref, d_ref, time_ref, out_ref, feat_terms_ref):
    total = (a_ref[...] + b_ref[...]) + (c_ref[...] + d_ref[...])
    out_ref[...] = total
    feat_count, time_count = feat_terms_ref.shape[1], time_ref.shape[1]
    cells = feat_count * time_count
    spread = exact(time_ref[...], one_hot_time(feat_count, time_count))
    feat_terms_ref[...] = exact(total[:, :cells] * spread, one_hot_feat(feat_count, time_count), NT)


def diagonal(square):
    kept = jnp.where(iota(square.shape, 0) == iota(square.shape, 1), square, 0.0)
    return jnp.sum(kept, axis=1, keepdims=True), jnp.sum(kept, axis=0, keepdims=True)


def norms(square):
    column, row = diagonal(square)
    return 1.0 / jnp.sqrt(column + epsilon), 1.0 / jnp.sqrt(row + epsilon)


def solve_feat(total_pat, a_ref, b_ref, t0_ref, t1_ref, t2_ref, t3_ref, time_gram_ref, raw_ref, sums_ref, gram_ref, scale_ref):
    rank, feat_count = raw_ref.shape
    cells = a_ref.shape[1] - LANES
    time_count = cells // feat_count
    gram = (a_ref[:, cells:] + b_ref[:, cells:])[:, :rank] / total_pat
    column, row = norms(gram)
    pat_gram = gram * column * row
    feat_terms = ((t0_ref[...] + t1_ref[...]) + (t2_ref[...] + t3_ref[...])) * column
    _, raw = eliminate([wide(pat_gram * time_gram_ref[...]), feat_terms])
    weighted = (a_ref[:, :cells] + b_ref[:, :cells]) * column
    spread = exact(raw, one_hot_feat(feat_count, time_count))
    time_terms = exact(weighted * spread, one_hot_time(feat_count, time_count), NT)
    raw_ref[...] = raw
    sums_ref[...] = wide(jnp.concatenate([exact(raw, raw, NT), time_terms], axis=1))
    gram_ref[...] = pat_gram
    scale_ref[...] = jnp.broadcast_to(column, scale_ref.shape)


def solve_time(total_pat, total_feat, a_ref, b_ref, raw_ref, gram_ref, feat_ref, time_ref):
    rank, time_count = time_ref.shape
    total = a_ref[...] + b_ref[...]
    gram = total[:, :rank] / total_feat
    column, row = norms(gram)
    feat_ref[...] = raw_ref[...] * column
    system = gram_ref[...] * (gram * column * row)
    terms = total[:, rank : rank + time_count] * column
    (solved,) = eliminate([wide(jnp.concatenate([system, terms], axis=1))])
    time_ref[...] = solved[:, rank : rank + time_count] * (1.0 / math.sqrt(total_pat * total_feat))


def scale_pat(own_ref, other_ref, scale_ref, out_ref):
    half = own_ref.shape[1]
    scale = scale_ref[:, :1]
    me = lax.axis_index("feat")
    out_ref[:, pl.ds(pl.multiple_of(me * half, half), half)] = own_ref[...] * scale
    out_ref[:, pl.ds(pl.multiple_of((1 - me) * half, half), half)] = other_ref[...] * scale


def per_device(tensor, feat_init, time_init):
    feat_dev, time_dev, rows_dev = tensor.shape
    rank = feat_init.shape[0]
    total_pat = rows_dev * lax.axis_size("pat")
    total_feat = feat_dev * lax.axis_size("feat")
    cells, half = feat_dev * time_dev, rows_dev // 2
    flat = tensor.reshape(cells, rows_dev)
    swap = [(0, 1), (1, 0)]

    def from_core(x):
        return lax.ppermute(x, "feat", swap)

    def from_tm(x):
        return lax.ppermute(x, "tm", swap)

    def from_pat(x, flip):
        return lax.ppermute(x, "pat", [(i, i ^ flip) for i in range(lax.axis_size("pat"))])

    def from_both(x, flip):
        count = 2 * lax.axis_size("pat")
        return lax.ppermute(x, ("pat", "tm"), [(i, i ^ (2 * flip + 1)) for i in range(count)])

    feat_other = from_core(feat_init)
    time_other = from_tm(time_init)

    sems = [pltpu.SemaphoreType.DMA((half // CHUNK,))]
    work = dict(flops=2 * 3 * rank * cells * half, moved=4 * cells * half)
    terms_for_core, kept_other, hl = call(
        first_half,
        [((rank, half), f32), ((cells, half), f32), ((2 * rank, cells), bf16)],
        "first_half", [VMEM, VMEM, HBM], sems, 44, **work,
    )(feat_init, time_init, flat)
    arrived = from_core(terms_for_core)
    hl, feat_other, time_other = lax.optimization_barrier((hl, feat_other, time_other))
    terms_own, kept_own = call(
        second_half, [((rank, half), f32), ((cells, half), f32)], "second_half", [VMEM, HBM], sems, 40, **work
    )(hl, flat)

    pieces = 2
    width = half // pieces
    mine = [terms_own[:, i * width : (i + 1) * width] + arrived[:, i * width : (i + 1) * width] for i in range(pieces)]
    theirs = [from_tm(x) for x in mine]
    inverse, time_gram = call(
        start_system, [((rank, rank), f32), ((rank, rank), f32)], "start_system", [VMEM] * 4, flops=2**21, moved=2**16
    )(feat_init, feat_other, time_init, time_other)
    (raw_own,) = call(solve_pat, [((rank, half), f32)], "solve_pat", [VMEM] * (1 + 2 * pieces), flops=2**26, moved=2**20)(
        inverse, *mine, *theirs
    )
    raw_other = from_core(raw_own)
    payload = [((rank, cells + LANES), f32)]
    (part,) = call(weigh, payload, "weigh_own", [VMEM] * 2, **work)(raw_own, kept_own)
    (part,) = call(weigh, payload, "weigh_other", [VMEM] * 3, **work)(raw_other, kept_other, part)

    x_parts = [from_pat(part, flip) for flip in (1, 2, 3)]
    (part,) = call(add_four, payload, "add_x", [VMEM] * 4, flops=2**18, moved=2**20)(part, *x_parts)
    y_parts = [from_pat(part, flip) for flip in (8, 16, 24)]
    part, feat_terms = call(
        add_and_project, payload + [((rank, feat_dev), f32)], "add_y", [VMEM] * 5, flops=2**26, moved=2**20
    )(part, *y_parts, time_init)
    part_hi = from_pat(part, 4)
    terms_hi = from_pat(feat_terms, 4)
    terms_tm = from_tm(feat_terms)
    terms_far = from_both(feat_terms, 4)
    feat_raw, sums, pat_gram, scale = call(
        lambda *refs: solve_feat(total_pat, *refs),
        [((rank, feat_dev), f32), ((rank, LANES), f32), ((rank, rank), f32), ((rank, LANES), f32)],
        "solve_feat", [VMEM] * 7, flops=2**26, moved=2**20,
    )(part, part_hi, feat_terms, terms_tm, terms_hi, terms_far, time_gram)
    sums_core = from_core(sums)
    (factor_pat,) = call(scale_pat, [((rank, rows_dev), f32)], "scale_pat", [VMEM] * 3, flops=2**18, moved=2**20)(
        raw_own, raw_other, scale
    )
    factor_feat, factor_time = call(
        lambda *refs: solve_time(total_pat, total_feat, *refs),
        [((rank, feat_dev), f32), ((rank, time_dev), f32)],
        "solve_time", [VMEM] * 4, flops=2**22, moved=2**17,
    )(sums, sums_core, feat_raw, pat_gram)
    return (factor_pat, factor_feat, factor_time)


def solution(mesh):
    placed = (P("feat", "tm", "pat"), P(None, "feat"), P(None, "tm"))
    return jax.shard_map(
        per_device,
        mesh=mesh,
        in_specs=placed,
        out_specs=(P(None, "pat"), P(None, "feat"), P(None, "tm")),
        check_vma=False,
    )
```

```python
import math

import jax
import jax.numpy as jnp
from jax import lax
from jax.experimental import pallas as pl
from jax.experimental.pallas import tpu as pltpu
from jax.sharding import PartitionSpec as P

f32, bf16 = jnp.float32, jnp.bfloat16
highest = lax.Precision.HIGHEST
epsilon = 1e-06
VMEM = pl.BlockSpec(memory_space=pltpu.VMEM)
HBM = pl.BlockSpec(memory_space=pltpu.HBM)
NN = (((1,), (0,)), ((), ()))
NT = (((1,), (1,)), ((), ()))
TN = (((0,), (0,)), ((), ()))
LANES = 128


def exact(a, b, dims=NN):
    return lax.dot_general(a, b, dims, precision=highest, preferred_element_type=f32)


def quick(a, b, dims=NN):
    return lax.dot_general(a, b, dims, preferred_element_type=f32)


def split(x):
    hi = x.astype(bf16)
    return hi, (x - hi.astype(f32)).astype(bf16)


def iota(shape, dim):
    return lax.broadcasted_iota(jnp.int32, shape, dim)


def one_hot_feat(feat, time):
    shape = (feat, feat * time)
    return jnp.where(lax.div(iota(shape, 1), time) == iota(shape, 0), 1.0, 0.0).astype(f32)


def one_hot_time(feat, time):
    shape = (time, feat * time)
    return jnp.where(lax.rem(iota(shape, 1), time) == iota(shape, 0), 1.0, 0.0).astype(f32)


def eliminate(tiles, group=8):
    rank = tiles[0].shape[0]
    rows = iota((rank, LANES), 0)
    for start in range(0, rank, group):
        columns = [
            jnp.broadcast_to(tiles[0][:, start + t : start + t + 1], (rank, LANES)) for t in range(group)
        ]
        for t in range(group):
            at = start + t
            column = columns[t]
            inverse = 1.0 / column[at : at + 1, :]
            here = rows == at
            for later in range(t + 1, group):
                scaled = columns[later][at : at + 1, :] * inverse
                columns[later] = jnp.where(here, scaled, columns[later] - column * scaled)
            new = []
            for tile in tiles:
                scaled = tile[at : at + 1, :] * inverse
                new.append(jnp.where(here, scaled, tile - column * scaled))
            tiles = new
    return tiles


def invert(system):
    rank = system.shape[0]
    eye = jnp.where(iota((rank, rank), 0) == iota((rank, rank), 1), 1.0, 0.0).astype(f32)
    (solved,) = eliminate([wide(jnp.concatenate([system, eye], axis=1))])
    return solved[:, rank : 2 * rank]


def wide(x, columns=LANES):
    return jnp.concatenate([x, jnp.zeros((x.shape[0], columns - x.shape[1]), f32)], axis=1)


def call(body, out_shape, name, specs, scratch=(), limit=24, flops=0, moved=0):
    return pl.pallas_call(
        body,
        out_shape=[jax.ShapeDtypeStruct(s, d) for s, d in out_shape],
        in_specs=specs,
        out_specs=[VMEM] * len(out_shape),
        scratch_shapes=list(scratch),
        compiler_params=pltpu.CompilerParams(vmem_limit_bytes=limit * 2**20),
        cost_estimate=pl.CostEstimate(flops=flops, bytes_accessed=moved, transcendentals=0),
        name=name,
    )


CHUNK = 256
DEPTH = 256
SHARES = (1280, 768)


def terms_of(hl_ref, block_ref, kept_ref, terms_ref, sems, first, build=None):
    rank = terms_ref.shape[0]
    cells, patients = kept_ref.shape
    copies = []
    for c in range(patients // CHUNK):
        start = pl.multiple_of(first + c * CHUNK, CHUNK)
        copies.append(
            pltpu.make_async_copy(
                block_ref.at[:, pl.ds(start, CHUNK)], kept_ref.at[:, pl.ds(c * CHUNK, CHUNK)], sems.at[c]
            )
        )
    for copy in copies:
        copy.start()
    if build is not None:
        build()
    for c, copy in enumerate(copies):
        copy.wait()
        total = None
        for d in range(0, cells, DEPTH):
            hi, lo = split(kept_ref[d : d + DEPTH, c * CHUNK : (c + 1) * CHUNK])
            both = quick(hl_ref[:, d : d + DEPTH], hi)
            part = both[:rank] + both[rank:] + quick(hl_ref[:rank, d : d + DEPTH], lo)
            total = part if total is None else total + part
        terms_ref[:, c * CHUNK : (c + 1) * CHUNK] = total


def factors(init):
    rank = init.shape[0] - 8
    return init[:rank, :], init[rank:, :rank]


def first_terms(half, offset, init_ref, block_ref, terms_ref, kept_ref, hl_ref, time_ref, sems):
    def build():
        feat, time = factors(init_ref[...])
        count = (feat.shape[1], time.shape[0])
        product = exact(feat, one_hot_feat(*count)) * exact(time, one_hot_time(*count), TN)
        hi, lo = split(product)
        hl_ref[...] = jnp.concatenate([hi, lo], axis=0)
        time_ref[...] = jnp.concatenate([init_ref[init_ref.shape[0] - 8 :, :]] * (time_ref.shape[1] // LANES), axis=1)

    other = 1 - lax.axis_index("feat")
    terms_of(hl_ref, block_ref, kept_ref, terms_ref, sems, other * half + offset, build)


def more_terms(mine, half, offset, hl_ref, before_ref, block_ref, terms_ref, kept_ref, sems):
    me = lax.axis_index("feat")
    terms_of(hl_ref, block_ref, kept_ref, terms_ref, sems, (me if mine else 1 - me) * half + offset)


def start_system(init_ref, core_ref, piece_ref, inverse_ref, time_gram_ref):
    rank = inverse_ref.shape[0]
    feat, time = factors(init_ref[...])
    feat_other, _ = factors(core_ref[...])
    time_other = piece_ref[rank:, :rank]
    time_gram = exact(time, time, TN) + exact(time_other, time_other, TN)
    system = (exact(feat, feat, NT) + exact(feat_other, feat_other, NT)) * time_gram
    inverse_ref[...] = invert(system)
    time_gram_ref[...] = time_gram


def add_piece(mine_ref, theirs_ref, *refs):
    out_ref = refs[-1]
    out_ref[...] = mine_ref[...] + theirs_ref[: mine_ref.shape[0], :]


def pack(square):
    return jnp.concatenate([square[i : i + 8, :] for i in range(0, 32, 8)], axis=1)


def unpack(packed):
    return jnp.concatenate([packed[:, i : i + 32] for i in range(0, 128, 32)], axis=0)


def weigh(columns, *refs):
    pairs, (*before, out_ref, gram_ref) = refs[: 2 * len(columns)], refs[2 * len(columns) :]
    rank = gram_ref.shape[0]
    total = gram = None
    for i, first in enumerate(columns):
        terms_ref, kept_ref = pairs[2 * i : 2 * i + 2]
        hi, lo = split(terms_ref[...])
        hl = jnp.concatenate([hi, lo], axis=0)
        for c in range(0, terms_ref.shape[1], DEPTH):
            kept_hi, kept_lo = split(kept_ref[:, first + c : first + c + DEPTH])
            both = quick(kept_hi, hl[:, c : c + DEPTH], NT)
            part = both[:, :rank] + both[:, rank:] + quick(kept_lo, hl[:rank, c : c + DEPTH], NT)
            total = part if total is None else total + part
        square = exact(terms_ref[...], terms_ref[...], NT)
        gram = square if gram is None else gram + square
    weighted = total.T
    if before:
        weighted, gram = weighted + before[0][...], gram + before[1][...]
    out_ref[...] = weighted
    gram_ref[...] = gram


def weigh_last(columns, *refs):
    *ins, q0, q1, q2, q3, total_ref, gram_ref = refs
    weigh(columns, *ins, total_ref, gram_ref)
    rank, cells = q0.shape[0] - 8, q0.shape[1]
    gram = wide(pack(gram_ref[...]), cells)
    me = lax.rem(lax.axis_index("pat"), 4)
    for flip, out_ref in enumerate((q0, q1, q2, q3)):
        first = pl.multiple_of(lax.bitwise_xor(me, flip) * cells, cells)
        out_ref[:rank, :] = total_ref[:, pl.ds(first, cells)]
        out_ref[rank:, :] = gram


def pair(a_ref, b_ref, *refs):
    refs[-1][...] = a_ref[...] + b_ref[...]


def hold(a_ref, first_ref, out_ref):
    out_ref[...] = a_ref[...]


def add_and_project(a_ref, b_ref, c_ref, init_ref, inverse_ref, out_ref, far_ref, tail_ref):
    total = a_ref[...] + (b_ref[...] + c_ref[...])
    cells = total.shape[1]
    rank, feat_count = init_ref.shape[0] - 8, 32
    inverse = inverse_ref[...]
    weighted = exact(inverse, total[:rank, :])
    gram = pack(exact(exact(inverse, unpack(total[rank:, :LANES])), inverse, NT))
    time_count = cells // feat_count
    _, time = factors(init_ref[...])
    spread = exact(time, one_hot_time(feat_count, time_count), TN)
    terms = pack(exact(weighted * spread, one_hot_feat(feat_count, time_count), NT))
    tails = jnp.concatenate([gram, terms], axis=1)
    out_ref[:rank, :] = weighted
    out_ref[rank:, :] = tails
    far_ref[...] = tails
    tail_ref[...] = terms


def diagonal(square):
    kept = jnp.where(iota(square.shape, 0) == iota(square.shape, 1), square, 0.0)
    return jnp.sum(kept, axis=1, keepdims=True), jnp.sum(kept, axis=0, keepdims=True)


def norms(square):
    column, row = diagonal(square)
    return 1.0 / jnp.sqrt(column + epsilon), 1.0 / jnp.sqrt(row + epsilon)


def feat_system(total_pat, own_ref, far_ref, inverse_ref, time_gram_ref, gram_ref, scaled_ref, scale_ref, solver_ref):
    gram = unpack(own_ref[:, :LANES] + far_ref[:, :LANES]) / total_pat
    column, row = norms(gram)
    pat_gram = gram * column * row
    gram_ref[...] = pat_gram
    scaled_ref[...] = inverse_ref[...] * column
    scale_ref[...] = jnp.broadcast_to(column, scale_ref.shape)
    solver_ref[...] = invert(pat_gram * time_gram_ref[...]) * row


def scale_weighted(own_ref, high_ref, scale_ref, solver_ref, out_ref):
    rank = out_ref.shape[0]
    out_ref[...] = (own_ref[:rank, :] + high_ref[:rank, :]) * scale_ref[:, :1]


def solve_feat(own_ref, far_ref, high_ref, tm_ref, weighted_ref, solver_ref, out_ref):
    rank, cells = weighted_ref.shape
    feat_count = 32
    time_count = cells // feat_count
    terms = (own_ref[:, LANES:] + tm_ref[...]) + (high_ref[rank:, LANES:] + far_ref[:, LANES:])
    raw = exact(solver_ref[...], unpack(terms))
    spread = exact(raw, one_hot_feat(feat_count, time_count))
    time_terms = exact(weighted_ref[...] * spread, one_hot_time(feat_count, time_count), NT)
    out_ref[:, :LANES] = wide(jnp.concatenate([exact(raw, raw, NT), time_terms], axis=1))
    here = lax.div(iota((rank, LANES), 1), feat_count) == lax.rem(lax.axis_index("pat"), 4)
    out_ref[:, LANES:] = jnp.where(here, jnp.concatenate([raw] * 4, axis=1), 0.0)


def solve_time(total_pat, total_feat, a_ref, b_ref, raw_ref, gram_ref, feat_ref, time_ref):
    time_count, rank = time_ref.shape
    total = a_ref[...] + b_ref[...]
    gram = total[:, :rank] / total_feat
    column, row = norms(gram)
    feat_ref[...] = raw_ref[...] * column
    system = gram_ref[...] * (gram * column * row)
    terms = total[:, rank : rank + time_count] * column
    (solved,) = eliminate([wide(jnp.concatenate([system, terms], axis=1))])
    place = jnp.where(iota((time_count, LANES), 1) == iota((time_count, LANES), 0) + rank, 1.0, 0.0).astype(f32)
    factor = exact(place, solved, NT)
    time_ref[...] = factor * (1.0 / math.sqrt(total_pat * total_feat))


def scale_pat(scaled_ref, *refs):
    *terms, out_ref, ran_ref = refs
    me = lax.axis_index("feat")
    half = out_ref.shape[1] // 2
    offset = 0
    for i, terms_ref in enumerate(terms):
        who = me if i % 2 == 0 else 1 - me
        patients = terms_ref.shape[1]
        first = pl.multiple_of(who * half + offset, CHUNK)
        out_ref[:, pl.ds(first, patients)] = exact(scaled_ref[...], terms_ref[...])
        offset += patients * (i % 2)
    ran_ref[...] = jnp.zeros(ran_ref.shape, f32)


def per_device(tensor, feat_init, time_init):
    feat_dev, time_dev, rows_dev = tensor.shape
    rank = feat_init.shape[0]
    total_pat = rows_dev * lax.axis_size("pat")
    total_feat = feat_dev * lax.axis_size("feat")
    cells, half = feat_dev * time_dev, rows_dev // 2
    flat = tensor.reshape(cells, rows_dev)
    swap = [(0, 1), (1, 0)]

    def from_core(x):
        return lax.ppermute(x, "feat", swap)

    def from_tm(x):
        return lax.ppermute(x, "tm", swap)

    def from_pat(x, flip):
        return lax.ppermute(x, "pat", [(i, i ^ flip) for i in range(lax.axis_size("pat"))])

    def from_both(x, flip):
        count = 2 * lax.axis_size("pat")
        return lax.ppermute(x, ("pat", "tm"), [(i, i ^ (2 * flip + 1)) for i in range(count)])

    square = ((rank, rank), f32)
    init = jnp.concatenate([feat_init, jnp.pad(time_init.T, ((0, 0), (0, feat_dev - rank)))], axis=0)

    def load(patients):
        return dict(flops=2 * 3 * rank * cells * patients, moved=4 * cells * patients)

    def bring(body, patients, name, *operands, more=()):
        return call(
            body, [((rank, patients), f32), ((cells, patients), f32), *more], name,
            [VMEM] * (len(operands) - 1) + [HBM], [pltpu.SemaphoreType.DMA((patients // CHUNK,))], 45, **load(patients),
        )(*operands)

    offset, before, kept, mine, theirs = 0, None, [], [], []
    for count, patients in enumerate(SHARES):
        if count == 0:
            away, kept_other, hl, time_rows = bring(
                lambda *refs: first_terms(half, 0, *refs), patients, "first_terms", init, flat,
                more=[((2 * rank, cells), bf16), ((8, patients), f32)],
            )
            arrived, init_core = lax.optimization_barrier((from_core(away), from_core(init)))
        else:
            away, kept_other = bring(
                lambda *refs, offset=offset: more_terms(False, half, offset, *refs), patients, "terms_for_core", hl, before, flat
            )
            arrived = from_core(away)
        before, kept_own = bring(
            lambda *refs, offset=offset: more_terms(True, half, offset, *refs), patients, "terms_own", hl, away, flat
        )
        mine.append(before + arrived)
        theirs.append(from_tm(jnp.concatenate([mine[0], time_rows], axis=0) if count == 0 else mine[-1]))
        kept.append((kept_own, kept_other))
        offset += patients

    packed = ((8, LANES), f32)
    payload = ((rank + 8, cells // 4), f32)
    summed = [((rank, cells), f32), square]
    few = dict(flops=2**20, moved=2**18)
    sofar, totals = (), []
    for count, patients in enumerate(SHARES):
        (total,) = call(add_piece, [((rank, patients), f32)], "add_piece", [VMEM] * 3, **few)(
            mine[count], theirs[count], *(sofar[1:] or [mine[-1]])
        )
        other = from_core(total)
        totals += [total, other]
        sofar = call(lambda *refs: weigh([0], *refs), summed, "weigh", [VMEM] * (2 + len(sofar)), **load(patients))(
            total, kept[count][0], *sofar
        )
        if count < len(SHARES) - 1:
            sofar = call(lambda *refs: weigh([0], *refs), summed, "weigh", [VMEM] * 4, **load(patients))(
                other, kept[count][1], *sofar
            )
    quarters = call(
        lambda *refs: weigh_last([0], *refs), [payload] * 4, "weigh_last", [VMEM] * 4,
        [pltpu.VMEM((rank, cells), f32), pltpu.VMEM((rank, rank), f32)], **load(patients)
    )(totals[-1], kept[-1][1], *sofar)
    inverse, time_gram = call(start_system, [square] * 2, "start_system", [VMEM] * 3, **few)(init, init_core, theirs[0])

    def over_ring(mine, third, second, first, shape, *after):
        (a,) = call(pair, [shape], "pair", [VMEM] * (2 + len(after)), **few)(mine, first, *after)
        (b,) = call(hold, [shape], "hold", [VMEM] * 2, **few)(second, a)
        return a, b, third

    a, b, c = over_ring(quarters[0], *[from_pat(quarters[i], i) for i in (1, 3, 2)], payload, inverse)
    part = a + (b + c)
    a, b, c = over_ring(part, *[from_pat(part, flip) for flip in (8, 24, 16)], payload)
    part, far_tail, tail = call(
        add_and_project, [payload, ((8, 2 * LANES), f32), packed], "add_and_project", [VMEM] * 5, **few
    )(a, b, c, init, inverse)
    far, high, tm = from_both(far_tail, 4), from_pat(part, 4), from_tm(tail)
    pat_gram, scaled, scale, solver = call(
        lambda *refs: feat_system(total_pat, *refs), [square, square, ((rank, LANES), f32), square], "feat_system", [VMEM] * 4, **few
    )(far_tail, far, inverse, time_gram)
    (weighted,) = call(scale_weighted, [((rank, cells // 4), f32)], "scale_weighted", [VMEM] * 4, **few)(
        part, high, scale, solver
    )
    double = ((rank, 2 * LANES), f32)
    (sums,) = call(solve_feat, [double], "solve_feat", [VMEM] * 6, **few)(far_tail, far, high, tm, weighted, solver)
    factor_pat, ran = call(scale_pat, [((rank, rows_dev), f32), packed], "scale_pat", [VMEM] * (1 + len(totals)), **few)(
        scaled, *totals
    )
    a, b, c = over_ring(sums, *[from_pat(sums, flip) for flip in (1, 3, 2)], double, ran)
    total = a + (b + c)
    sums, feat_raw = total[:, :LANES], total[:, LANES:]
    factor_feat, factor_time = call(
        lambda *refs: solve_time(total_pat, total_feat, *refs),
        [((rank, feat_dev), f32), ((time_dev, rank), f32)],
        "solve_time", [VMEM] * 4, **few,
    )(sums, from_core(sums), feat_raw, pat_gram)
    return (factor_pat, factor_feat, factor_time.T)


def solution(mesh):
    placed = (P("feat", "tm", "pat"), P(None, "feat"), P(None, "tm"))
    return jax.shard_map(
        per_device,
        mesh=mesh,
        in_specs=placed,
        out_specs=(P(None, "pat"), P(None, "feat"), P(None, "tm")),
        check_vma=False,
    )
```

```python
import math

import jax
import jax.numpy as jnp
from jax import lax
from jax.experimental import pallas as pl
from jax.experimental.pallas import tpu as pltpu
from jax.sharding import PartitionSpec as P

f32, bf16 = jnp.float32, jnp.bfloat16
highest = lax.Precision.HIGHEST
epsilon = 1e-06
VMEM = pl.BlockSpec(memory_space=pltpu.VMEM)
HBM = pl.BlockSpec(memory_space=pltpu.HBM)
NN = (((1,), (0,)), ((), ()))
NT = (((1,), (1,)), ((), ()))
TN = (((0,), (0,)), ((), ()))
LANES = 128


def exact(a, b, dims=NN):
    return lax.dot_general(a, b, dims, precision=highest, preferred_element_type=f32)


def quick(a, b, dims=NN):
    return lax.dot_general(a, b, dims, preferred_element_type=f32)


def split(x):
    hi = x.astype(bf16)
    return hi, (x - hi.astype(f32)).astype(bf16)


def iota(shape, dim):
    return lax.broadcasted_iota(jnp.int32, shape, dim)


def one_hot_feat(feat, time):
    shape = (feat, feat * time)
    return jnp.where(lax.div(iota(shape, 1), time) == iota(shape, 0), 1.0, 0.0).astype(f32)


def one_hot_time(feat, time):
    shape = (time, feat * time)
    return jnp.where(lax.rem(iota(shape, 1), time) == iota(shape, 0), 1.0, 0.0).astype(f32)


def eliminate(tiles, group=8):
    rank = tiles[0].shape[0]
    rows = iota((rank, LANES), 0)
    for start in range(0, rank, group):
        columns = [
            jnp.broadcast_to(tiles[0][:, start + t : start + t + 1], (rank, LANES)) for t in range(group)
        ]
        for t in range(group):
            at = start + t
            column = columns[t]
            inverse = 1.0 / column[at : at + 1, :]
            here = rows == at
            for later in range(t + 1, group):
                scaled = columns[later][at : at + 1, :] * inverse
                columns[later] = jnp.where(here, scaled, columns[later] - column * scaled)
            new = []
            for tile in tiles:
                scaled = tile[at : at + 1, :] * inverse
                new.append(jnp.where(here, scaled, tile - column * scaled))
            tiles = new
    return tiles


def invert(system):
    rank = system.shape[0]
    eye = jnp.where(iota((rank, rank), 0) == iota((rank, rank), 1), 1.0, 0.0).astype(f32)
    (solved,) = eliminate([wide(jnp.concatenate([system, eye], axis=1))])
    return solved[:, rank : 2 * rank]


def wide(x, columns=LANES):
    return jnp.concatenate([x, jnp.zeros((x.shape[0], columns - x.shape[1]), f32)], axis=1)


def call(body, out_shape, name, specs, scratch=(), limit=24, flops=0, moved=0):
    return pl.pallas_call(
        body,
        out_shape=[jax.ShapeDtypeStruct(s, d) for s, d in out_shape],
        in_specs=specs,
        out_specs=[VMEM] * len(out_shape),
        scratch_shapes=list(scratch),
        compiler_params=pltpu.CompilerParams(vmem_limit_bytes=limit * 2**20),
        cost_estimate=pl.CostEstimate(flops=flops, bytes_accessed=moved, transcendentals=0),
        name=name,
    )


CHUNK = 256
SHARES = (1024, 1024)
LOADS = 8
ROOM = 45


def terms_of(mine, half, offset, hl_ref, block_ref, terms_ref, kept_ref, sems, build=None):
    rank, patients = terms_ref.shape
    cells = kept_ref.shape[0]
    me = lax.axis_index("feat")
    first = pl.multiple_of((me if mine else 1 - me) * half + offset, CHUNK)
    step = cells // LOADS
    copies = []
    for i in range(LOADS):
        rows = pl.ds(i * step, step)
        copies.append(
            pltpu.make_async_copy(block_ref.at[rows, pl.ds(first, patients)], kept_ref.at[rows, :], sems.at[i])
        )
    for copy in copies:
        copy.start()
    if build is not None:
        build()
    for i, copy in enumerate(copies):
        copy.wait()
        rows = slice(i * step, (i + 1) * step)
        for c in range(0, patients, CHUNK):
            hi, lo = split(kept_ref[rows, c : c + CHUNK])
            both = quick(hl_ref[:, rows], hi)
            part = both[:rank] + both[rank:] + quick(hl_ref[:rank, rows], lo)
            if i > 0:
                part = part + terms_ref[:, c : c + CHUNK]
            terms_ref[:, c : c + CHUNK] = part


def first_terms(half, init_ref, block_ref, terms_ref, kept_ref, hl_ref, time_out_ref, sems):
    def build():
        rank = terms_ref.shape[0]
        feat, time = init_ref[:rank, :], init_ref[rank:, :rank]
        count = (feat.shape[1], time.shape[0])
        product = exact(feat, one_hot_feat(*count)) * exact(time, one_hot_time(*count), TN)
        hl_ref[...] = jnp.concatenate(split(product), axis=0)
        time_out_ref[...] = jnp.concatenate([wide(time)] * (time_out_ref.shape[1] // LANES), axis=1)

    terms_of(False, half, 0, hl_ref, block_ref, terms_ref, kept_ref, sems, build)


def more_terms(mine, half, offset, hl_ref, before_ref, block_ref, terms_ref, kept_ref, sems):
    terms_of(mine, half, offset, hl_ref, block_ref, terms_ref, kept_ref, sems)


def start_system(init_ref, core_ref, piece_ref, inverse_ref, time_gram_ref):
    rank = inverse_ref.shape[0]
    feat, feat_other = init_ref[:rank, :], core_ref[:rank, :]
    time, time_other = init_ref[rank:, :rank], piece_ref[rank:, :rank]
    time_gram = exact(time, time, TN) + exact(time_other, time_other, TN)
    system = (exact(feat, feat, NT) + exact(feat_other, feat_other, NT)) * time_gram
    inverse_ref[...] = invert(system)
    time_gram_ref[...] = time_gram


def solve_pat(inverse_ref, *refs):
    count = len(refs) // 2
    for terms_ref, out_ref in zip(refs[:count], refs[count:]):
        out_ref[...] = exact(inverse_ref[...], terms_ref[...])
    refs[-1][...] = jnp.zeros(refs[-1].shape, f32)


def add_piece(mine_ref, theirs_ref, *refs):
    out_ref = refs[-1]
    out_ref[...] = mine_ref[...] + theirs_ref[: mine_ref.shape[0], :]


def pack(square):
    return jnp.concatenate([square[i : i + 8, :] for i in range(0, 32, 8)], axis=1)


def unpack(packed):
    return jnp.concatenate([packed[:, i : i + 32] for i in range(0, 128, 32)], axis=0)


def weigh(columns, *refs):
    pairs, (*before, out_ref, gram_ref) = refs[: 2 * len(columns)], refs[2 * len(columns) :]
    rank = gram_ref.shape[0]
    total = gram = None
    for i, first in enumerate(columns):
        terms_ref, kept_ref = pairs[2 * i : 2 * i + 2]
        hi, lo = split(terms_ref[...])
        hl = jnp.concatenate([hi, lo], axis=0)
        for c in range(0, terms_ref.shape[1], CHUNK):
            kept_hi, kept_lo = split(kept_ref[:, first + c : first + c + CHUNK])
            both = quick(kept_hi, hl[:, c : c + CHUNK], NT)
            part = both[:, :rank] + both[:, rank:] + quick(kept_lo, hl[:rank, c : c + CHUNK], NT)
            total = part if total is None else total + part
        square = exact(terms_ref[...], terms_ref[...], NT)
        gram = square if gram is None else gram + square
    weighted = total.T
    if before:
        weighted, gram = weighted + before[0][...], gram + before[1][...]
    out_ref[...] = weighted
    gram_ref[...] = gram


def weigh_last(columns, *refs):
    *ins, q0, q1, q2, q3, total_ref, gram_ref = refs
    weigh(columns, *ins, total_ref, gram_ref)
    rank, cells = q0.shape[0] - 8, q0.shape[1]
    gram = wide(pack(gram_ref[...]), cells)
    me = lax.rem(lax.axis_index("pat"), 4)
    for flip, out_ref in enumerate((q0, q1, q2, q3)):
        first = pl.multiple_of(lax.bitwise_xor(me, flip) * cells, cells)
        out_ref[:rank, :] = total_ref[:, pl.ds(first, cells)]
        out_ref[rank:, :] = gram


def pair(a_ref, b_ref, *refs):
    refs[-1][...] = a_ref[...] + b_ref[...]


def hold(a_ref, first_ref, out_ref):
    out_ref[...] = a_ref[...]


def add_and_project(a_ref, b_ref, c_ref, time_ref, inverse_ref, out_ref, tail_ref):
    total = a_ref[...] + (b_ref[...] + c_ref[...])
    cells = total.shape[1]
    rank, feat_count = inverse_ref.shape[0], 32
    inverse = inverse_ref[...]
    weighted = exact(inverse, total[:rank, :])
    gram = pack(exact(exact(inverse, unpack(total[rank:, :LANES])), inverse, NT))
    time_count = cells // feat_count
    time = time_ref[:, :rank]
    spread = exact(time, one_hot_time(feat_count, time_count), TN)
    terms = pack(exact(weighted * spread, one_hot_feat(feat_count, time_count), NT))
    out_ref[:rank, :] = weighted
    out_ref[rank:, :] = jnp.concatenate([gram, terms], axis=1)
    tail_ref[...] = terms


def diagonal(square):
    kept = jnp.where(iota(square.shape, 0) == iota(square.shape, 1), square, 0.0)
    return jnp.sum(kept, axis=1, keepdims=True), jnp.sum(kept, axis=0, keepdims=True)


def norms(square):
    column, row = diagonal(square)
    return 1.0 / jnp.sqrt(column + epsilon), 1.0 / jnp.sqrt(row + epsilon)


def feat_system(total_pat, own_ref, far_ref, time_gram_ref, gram_ref, scale_ref, solver_ref):
    rank = gram_ref.shape[0]
    gram = unpack(own_ref[rank:, :LANES] + far_ref[rank:, :LANES]) / total_pat
    column, row = norms(gram)
    pat_gram = gram * column * row
    gram_ref[...] = pat_gram
    scale_ref[...] = jnp.broadcast_to(column, scale_ref.shape)
    solver_ref[...] = invert(pat_gram * time_gram_ref[...]) * row


def scale_weighted(own_ref, high_ref, scale_ref, solver_ref, out_ref):
    rank = out_ref.shape[0]
    out_ref[...] = (own_ref[:rank, :] + high_ref[:rank, :]) * scale_ref[:, :1]


def solve_feat(own_ref, far_ref, high_ref, tm_ref, weighted_ref, solver_ref, out_ref):
    rank, cells = weighted_ref.shape
    feat_count = 32
    time_count = cells // feat_count
    terms = (own_ref[rank:, LANES:] + tm_ref[...]) + (high_ref[rank:, LANES:] + far_ref[rank:, LANES:])
    raw = exact(solver_ref[...], unpack(terms))
    spread = exact(raw, one_hot_feat(feat_count, time_count))
    time_terms = exact(weighted_ref[...] * spread, one_hot_time(feat_count, time_count), NT)
    out_ref[:, :LANES] = wide(jnp.concatenate([exact(raw, raw, NT), time_terms], axis=1))
    here = lax.div(iota((rank, LANES), 1), feat_count) == lax.rem(lax.axis_index("pat"), 4)
    out_ref[:, LANES:] = jnp.where(here, jnp.concatenate([raw] * 4, axis=1), 0.0)


def solve_time(total_pat, total_feat, a_ref, b_ref, raw_ref, gram_ref, feat_ref, time_ref):
    time_count, rank = time_ref.shape
    total = a_ref[...] + b_ref[...]
    gram = total[:, :rank] / total_feat
    column, row = norms(gram)
    feat_ref[...] = raw_ref[...] * column
    system = gram_ref[...] * (gram * column * row)
    terms = total[:, rank : rank + time_count] * column
    (solved,) = eliminate([wide(jnp.concatenate([system, terms], axis=1))])
    place = jnp.where(iota((time_count, LANES), 1) == iota((time_count, LANES), 0) + rank, 1.0, 0.0).astype(f32)
    factor = exact(place, solved, NT)
    time_ref[...] = factor * (1.0 / math.sqrt(total_pat * total_feat))


def scale_pat(scale_ref, *refs):
    *raws, out_ref, ran_ref = refs
    me = lax.axis_index("feat")
    half = out_ref.shape[1] // 2
    offset = 0
    for i, raw_ref in enumerate(raws):
        who = me if i % 2 == 0 else 1 - me
        patients = raw_ref.shape[1]
        first = pl.multiple_of(who * half + offset, CHUNK)
        out_ref[:, pl.ds(first, patients)] = raw_ref[...] * scale_ref[:, :1]
        offset += patients * (i % 2)
    ran_ref[...] = jnp.zeros(ran_ref.shape, f32)


def per_device(tensor, feat_init, time_init):
    feat_dev, time_dev, rows_dev = tensor.shape
    rank = feat_init.shape[0]
    total_pat = rows_dev * lax.axis_size("pat")
    total_feat = feat_dev * lax.axis_size("feat")
    cells, half = feat_dev * time_dev, rows_dev // 2
    flat = tensor.reshape(cells, rows_dev)
    swap = [(0, 1), (1, 0)]

    def from_core(x):
        return lax.ppermute(x, "feat", swap)

    def from_tm(x):
        return lax.ppermute(x, "tm", swap)

    def from_pat(x, flip):
        return lax.ppermute(x, "pat", [(i, i ^ flip) for i in range(lax.axis_size("pat"))])

    def from_both(x, flip):
        count = 2 * lax.axis_size("pat")
        return lax.ppermute(x, ("pat", "tm"), [(i, i ^ (2 * flip + 1)) for i in range(count)])

    square = ((rank, rank), f32)

    def load(patients):
        return dict(flops=patients, moved=patients)

    def bring(body, patients, name, *operands, more=()):
        return call(
            body, [((rank, patients), f32), ((cells, patients), f32), *more], name,
            [VMEM] * (len(operands) - 1) + [HBM], [pltpu.SemaphoreType.DMA((LOADS,))], ROOM, **load(patients),
        )(*operands)

    init = jnp.concatenate([feat_init, jnp.pad(time_init.T, ((0, 0), (0, feat_dev - rank)))], axis=0)
    c0, c1 = SHARES
    away_0, kept_o0, hl, time_rows = bring(
        lambda *refs: first_terms(half, *refs), c0, "first_terms", init, flat,
        more=[((2 * rank, cells), bf16), ((8, c0), f32)],
    )
    arrived_0, init_core = lax.optimization_barrier((from_core(away_0), from_core(init)))
    own_0, kept_m0 = bring(lambda *refs: more_terms(True, half, 0, *refs), c0, "terms_own", hl, away_0, flat)
    mine = [own_0 + arrived_0]
    theirs = [from_tm(jnp.concatenate([mine[0], time_rows], axis=0))]
    away_1, kept_o1 = bring(lambda *refs: more_terms(False, half, c0, *refs), c1, "terms_for_core", hl, own_0, flat)
    arrived_1 = from_core(away_1)
    own_1, kept_m1 = bring(lambda *refs: more_terms(True, half, c0, *refs), c1, "terms_own", hl, away_1, flat)
    mine.append(own_1 + arrived_1)
    theirs.append(from_tm(mine[1]))
    kept = [(kept_m0, kept_o0), (kept_m1, kept_o1)]

    packed = ((8, LANES), f32)
    payload = ((rank + 8, cells // 4), f32)
    summed = [((rank, cells), f32), square]
    few = dict(flops=2**20, moved=2**18)
    sofar, totals = (), []
    for count, patients in enumerate(SHARES):
        (total,) = call(add_piece, [((rank, patients), f32)], "add_piece", [VMEM] * 3, **few)(
            mine[count], theirs[count], *(sofar[1:] or [mine[-1]])
        )
        other = from_core(total)
        totals += [total, other]
        sofar = call(lambda *refs: weigh([0], *refs), summed, "weigh", [VMEM] * (2 + len(sofar)), **dict(flops=10 * 6 * rank * cells * patients, moved=40 * cells * patients))(
            total, kept[count][0], *sofar
        )
        if count < len(SHARES) - 1:
            sofar = call(lambda *refs: weigh([0], *refs), summed, "weigh", [VMEM] * 4, **dict(flops=10 * 6 * rank * cells * patients, moved=40 * cells * patients))(
                other, kept[count][1], *sofar
            )
    quarters = call(
        lambda *refs: weigh_last([0], *refs), [payload] * 4, "weigh_last", [VMEM] * 4,
        [pltpu.VMEM((rank, cells), f32), pltpu.VMEM((rank, rank), f32)], **dict(flops=10 * 6 * rank * cells * patients, moved=40 * cells * patients)
    )(totals[-1], kept[-1][1], *sofar)
    inverse, time_gram = call(start_system, [square] * 2, "start_system", [VMEM] * 3, **few)(
        init, init_core, theirs[0]
    )

    def over_ring(mine, third, second, first, shape, *after):
        (a,) = call(pair, [shape], "pair", [VMEM] * (2 + len(after)), **few)(mine, first, *after)
        (b,) = call(hold, [shape], "hold", [VMEM] * 2, **few)(second, a)
        return a, b, third

    a, b, c = over_ring(quarters[0], *[from_pat(quarters[i], i) for i in (1, 3, 2)], payload, inverse)
    part = a + (b + c)
    raws = [((rank, x.shape[1]), f32) for x in totals]
    *raws, solved = call(solve_pat, raws + [packed], "solve_pat", [VMEM] * (1 + len(totals)), **few)(inverse, *totals)
    a, b, c = over_ring(part, *[from_pat(part, flip) for flip in (8, 24, 16)], payload, solved)
    part, tail = call(add_and_project, [payload, packed], "add_and_project", [VMEM] * 5, **few)(a, b, c, time_rows, inverse)
    far, high, tm = from_both(part, 4), from_pat(part, 4), from_tm(tail)
    pat_gram, scale, solver = call(
        lambda *refs: feat_system(total_pat, *refs), [square, ((rank, LANES), f32), square], "feat_system", [VMEM] * 3, **few
    )(part, far, time_gram)
    (weighted,) = call(scale_weighted, [((rank, cells // 4), f32)], "scale_weighted", [VMEM] * 4, **few)(
        part, high, scale, solver
    )
    double = ((rank, 2 * LANES), f32)
    (sums,) = call(solve_feat, [double], "solve_feat", [VMEM] * 6, **few)(part, far, high, tm, weighted, solver)
    factor_pat, ran = call(scale_pat, [((rank, rows_dev), f32), packed], "scale_pat", [VMEM] * (1 + len(raws)), **few)(
        scale, *raws
    )
    a, b, c = over_ring(sums, *[from_pat(sums, flip) for flip in (1, 3, 2)], double, ran)
    total = a + (b + c)
    sums, feat_raw = total[:, :LANES], total[:, LANES:]
    factor_feat, factor_time = call(
        lambda *refs: solve_time(total_pat, total_feat, *refs),
        [((rank, feat_dev), f32), ((time_dev, rank), f32)],
        "solve_time", [VMEM] * 4, **few,
    )(sums, from_core(sums), feat_raw, pat_gram)
    return (factor_pat, factor_feat, factor_time.T)


def solution(mesh):
    placed = (P("feat", "tm", "pat"), P(None, "feat"), P(None, "tm"))
    return jax.shard_map(
        per_device,
        mesh=mesh,
        in_specs=placed,
        out_specs=(P(None, "pat"), P(None, "feat"), P(None, "tm")),
        check_vma=False,
    )
```

```python
import math

import jax
import jax.numpy as jnp
from jax import lax
from jax.experimental import pallas as pl
from jax.experimental.pallas import tpu as pltpu
from jax.sharding import PartitionSpec as P

f32, bf16 = jnp.float32, jnp.bfloat16
highest = lax.Precision.HIGHEST
epsilon = 1e-06
VMEM = pl.BlockSpec(memory_space=pltpu.VMEM)
HBM = pl.BlockSpec(memory_space=pltpu.HBM)
NN = (((1,), (0,)), ((), ()))
NT = (((1,), (1,)), ((), ()))
TN = (((0,), (0,)), ((), ()))
LANES = 128


def exact(a, b, dims=NN):
    return lax.dot_general(a, b, dims, precision=highest, preferred_element_type=f32)


def quick(a, b, dims=NN):
    return lax.dot_general(a, b, dims, preferred_element_type=f32)


def split(x):
    hi = x.astype(bf16)
    return hi, (x - hi.astype(f32)).astype(bf16)


def iota(shape, dim):
    return lax.broadcasted_iota(jnp.int32, shape, dim)


def one_hot_feat(feat, time):
    shape = (feat, feat * time)
    return jnp.where(lax.div(iota(shape, 1), time) == iota(shape, 0), 1.0, 0.0).astype(f32)


def one_hot_time(feat, time):
    shape = (time, feat * time)
    return jnp.where(lax.rem(iota(shape, 1), time) == iota(shape, 0), 1.0, 0.0).astype(f32)


def eliminate(tiles, group=8):
    rank = tiles[0].shape[0]
    rows = iota((rank, LANES), 0)
    for start in range(0, rank, group):
        columns = [
            jnp.broadcast_to(tiles[0][:, start + t : start + t + 1], (rank, LANES)) for t in range(group)
        ]
        for t in range(group):
            at = start + t
            column = columns[t]
            inverse = 1.0 / column[at : at + 1, :]
            here = rows == at
            for later in range(t + 1, group):
                scaled = columns[later][at : at + 1, :] * inverse
                columns[later] = jnp.where(here, scaled, columns[later] - column * scaled)
            new = []
            for tile in tiles:
                scaled = tile[at : at + 1, :] * inverse
                new.append(jnp.where(here, scaled, tile - column * scaled))
            tiles = new
    return tiles


def invert(system):
    rank = system.shape[0]
    eye = jnp.where(iota((rank, rank), 0) == iota((rank, rank), 1), 1.0, 0.0).astype(f32)
    (solved,) = eliminate([wide(jnp.concatenate([system, eye], axis=1))])
    return solved[:, rank : 2 * rank]


def wide(x, columns=LANES):
    return jnp.concatenate([x, jnp.zeros((x.shape[0], columns - x.shape[1]), f32)], axis=1)


def call(body, out_shape, name, specs, scratch=(), limit=24, flops=0, moved=0):
    return pl.pallas_call(
        body,
        out_shape=[jax.ShapeDtypeStruct(s, d) for s, d in out_shape],
        in_specs=specs,
        out_specs=[VMEM] * len(out_shape),
        scratch_shapes=list(scratch),
        compiler_params=pltpu.CompilerParams(vmem_limit_bytes=limit * 2**20),
        cost_estimate=pl.CostEstimate(flops=flops, bytes_accessed=moved, transcendentals=0),
        name=name,
    )


CHUNK = 256
SHARES = (1024, 1024)
LOADS = 4
ROOM = 40


def bring(half, mine, offset, *refs):
    refs = list(refs)
    sems = refs.pop() if mine is not None else None
    copies = []
    if mine is not None:
        build, there = {2: (False, False), 5: (False, True), 8: (True, True)}[len(refs)]
    else:
        build, there = False, True
    source = refs[: 2 * build + (there and not build)]
    refs = refs[len(source) :]
    there_ref = refs.pop(0) if there else None
    if mine is not None:
        block_ref, refs = refs[0], refs[1:]
        kept_ref = refs.pop(1 if there else 0)
        me = lax.axis_index("feat")
        first = pl.multiple_of((me if mine else 1 - me) * half + offset, CHUNK)
        cells, patients = kept_ref.shape
        step = cells // LOADS
        for i in range(LOADS):
            rows = pl.ds(i * step, step)
            copies.append(
                pltpu.make_async_copy(block_ref.at[rows, pl.ds(first, patients)], kept_ref.at[rows, :], sems.at[i])
            )
        for copy in copies:
            copy.start()
    if there:
        terms_ref = refs[0]
        rank, patients = terms_ref.shape
        if build:
            feat, time = source[0][...], source[1][...]
            hl_ref, time_ref = refs[1:]
            count = (feat.shape[1], time.shape[0])
            product = exact(feat, one_hot_feat(*count)) * exact(time, one_hot_time(*count), TN)
            hl_ref[...] = jnp.concatenate(split(product), axis=0)
            below = jnp.zeros((rank - time.shape[0], LANES), f32)
            time_ref[...] = jnp.concatenate([wide(time), below], axis=0)
        else:
            hl_ref = source[0]

        def contract(columns):
            total = None
            for d in range(0, there_ref.shape[0], CHUNK):
                hi, lo = split(there_ref[d : d + CHUNK, columns])
                both = quick(hl_ref[:, d : d + CHUNK], hi)
                part = both[:rank] + both[rank:] + quick(hl_ref[:rank, d : d + CHUNK], lo)
                total = part if total is None else total + part
            terms_ref[:, columns] = total

        if copies:
            @pl.loop(0, patients // CHUNK)
            def _(c):
                contract(pl.ds(pl.multiple_of(c * CHUNK, CHUNK), CHUNK))

        else:
            for c in range(0, patients, CHUNK):
                contract(slice(c, c + CHUNK))
    for copy in copies:
        copy.wait()


def start_system(feat_ref, core_ref, time_ref, piece_ref, inverse_ref, time_gram_ref):
    rank = inverse_ref.shape[0]
    feat, feat_other = feat_ref[...], core_ref[...]
    time, time_other = time_ref[...], piece_ref[:, piece_ref.shape[1] - LANES :]
    time_gram = (exact(time, time, TN) + exact(time_other, time_other, TN))[:rank, :rank]
    system = (exact(feat, feat, NT) + exact(feat_other, feat_other, NT)) * time_gram
    inverse_ref[...] = invert(system)
    time_gram_ref[...] = time_gram


def solve_pat(inverse_ref, *refs):
    count = len(refs) // 2
    for terms_ref, out_ref in zip(refs[:count], refs[count:]):
        out_ref[...] = exact(inverse_ref[...], terms_ref[...])
    refs[-1][...] = jnp.zeros(refs[-1].shape, f32)


def add_piece(mine_ref, theirs_ref, *refs):
    out_ref = refs[-1]
    out_ref[...] = mine_ref[...] + theirs_ref[:, : mine_ref.shape[1]]


def pack(square):
    return jnp.concatenate([square[i : i + 8, :] for i in range(0, 32, 8)], axis=1)


def unpack(packed):
    return jnp.concatenate([packed[:, i : i + 32] for i in range(0, 128, 32)], axis=0)


def weigh(columns, *refs):
    pairs, (*before, out_ref, gram_ref) = refs[: 2 * len(columns)], refs[2 * len(columns) :]
    rank = gram_ref.shape[0]
    total = gram = None
    for i, first in enumerate(columns):
        terms_ref, kept_ref = pairs[2 * i : 2 * i + 2]
        hi, lo = split(terms_ref[...])
        hl = jnp.concatenate([hi, lo], axis=0)
        for c in range(0, terms_ref.shape[1], CHUNK):
            kept_hi, kept_lo = split(kept_ref[:, first + c : first + c + CHUNK])
            both = quick(kept_hi, hl[:, c : c + CHUNK], NT)
            part = both[:, :rank] + both[:, rank:] + quick(kept_lo, hl[:rank, c : c + CHUNK], NT)
            total = part if total is None else total + part
        square = exact(terms_ref[...], terms_ref[...], NT)
        gram = square if gram is None else gram + square
    weighted = total.T
    if before:
        weighted, gram = weighted + before[0][...], gram + before[1][...]
    out_ref[...] = weighted
    gram_ref[...] = gram


def weigh_last(columns, *refs):
    *ins, q0, q1, q2, q3, total_ref, gram_ref = refs
    weigh(columns, *ins, total_ref, gram_ref)
    rank, cells = q0.shape[0] - 8, q0.shape[1]
    gram = wide(pack(gram_ref[...]), cells)
    me = lax.rem(lax.axis_index("pat"), 4)
    for flip, out_ref in enumerate((q0, q1, q2, q3)):
        first = pl.multiple_of(lax.bitwise_xor(me, flip) * cells, cells)
        out_ref[:rank, :] = total_ref[:, pl.ds(first, cells)]
        out_ref[rank:, :] = gram


def pair(a_ref, b_ref, *refs):
    refs[-1][...] = a_ref[...] + b_ref[...]


def hold(a_ref, first_ref, out_ref):
    out_ref[...] = a_ref[...]


def add_and_project(a_ref, b_ref, c_ref, time_ref, inverse_ref, out_ref, tail_ref):
    total = a_ref[...] + (b_ref[...] + c_ref[...])
    cells = total.shape[1]
    rank, feat_count = inverse_ref.shape[0], 32
    inverse = inverse_ref[...]
    weighted = exact(inverse, total[:rank, :])
    gram = pack(exact(exact(inverse, unpack(total[rank:, :LANES])), inverse, NT))
    time_count = cells // feat_count
    time = time_ref[:time_count, :rank]
    spread = exact(time, one_hot_time(feat_count, time_count), TN)
    terms = pack(exact(weighted * spread, one_hot_feat(feat_count, time_count), NT))
    out_ref[:rank, :] = weighted
    out_ref[rank:, :] = jnp.concatenate([gram, terms], axis=1)
    tail_ref[...] = terms


def diagonal(square):
    kept = jnp.where(iota(square.shape, 0) == iota(square.shape, 1), square, 0.0)
    return jnp.sum(kept, axis=1, keepdims=True), jnp.sum(kept, axis=0, keepdims=True)


def norms(square):
    column, row = diagonal(square)
    return 1.0 / jnp.sqrt(column + epsilon), 1.0 / jnp.sqrt(row + epsilon)


def feat_system(total_pat, own_ref, far_ref, time_gram_ref, gram_ref, scale_ref, solver_ref):
    rank = gram_ref.shape[0]
    gram = unpack(own_ref[rank:, :LANES] + far_ref[rank:, :LANES]) / total_pat
    column, row = norms(gram)
    pat_gram = gram * column * row
    gram_ref[...] = pat_gram
    scale_ref[...] = jnp.broadcast_to(column, scale_ref.shape)
    solver_ref[...] = invert(pat_gram * time_gram_ref[...]) * row


def scale_weighted(own_ref, high_ref, scale_ref, solver_ref, out_ref):
    rank = out_ref.shape[0]
    out_ref[...] = (own_ref[:rank, :] + high_ref[:rank, :]) * scale_ref[:, :1]


def solve_feat(own_ref, far_ref, high_ref, tm_ref, weighted_ref, solver_ref, out_ref):
    rank, cells = weighted_ref.shape
    feat_count = 32
    time_count = cells // feat_count
    terms = (own_ref[rank:, LANES:] + tm_ref[...]) + (high_ref[rank:, LANES:] + far_ref[rank:, LANES:])
    raw = exact(solver_ref[...], unpack(terms))
    spread = exact(raw, one_hot_feat(feat_count, time_count))
    time_terms = exact(weighted_ref[...] * spread, one_hot_time(feat_count, time_count), NT)
    out_ref[:, :LANES] = wide(jnp.concatenate([exact(raw, raw, NT), time_terms], axis=1))
    here = lax.div(iota((rank, LANES), 1), feat_count) == lax.rem(lax.axis_index("pat"), 4)
    out_ref[:, LANES:] = jnp.where(here, jnp.concatenate([raw] * 4, axis=1), 0.0)


def solve_time(total_pat, total_feat, a_ref, b_ref, raw_ref, gram_ref, feat_ref, time_ref):
    time_count, rank = time_ref.shape
    total = a_ref[...] + b_ref[...]
    gram = total[:, :rank] / total_feat
    column, row = norms(gram)
    feat_ref[...] = raw_ref[...] * column
    system = gram_ref[...] * (gram * column * row)
    terms = total[:, rank : rank + time_count] * column
    (solved,) = eliminate([wide(jnp.concatenate([system, terms], axis=1))])
    place = jnp.where(iota((time_count, LANES), 1) == iota((time_count, LANES), 0) + rank, 1.0, 0.0).astype(f32)
    factor = exact(place, solved, NT)
    time_ref[...] = factor * (1.0 / math.sqrt(total_pat * total_feat))


def scale_pat(scale_ref, *refs):
    *raws, out_ref, ran_ref = refs
    me = lax.axis_index("feat")
    half = out_ref.shape[1] // 2
    offset = 0
    for i, raw_ref in enumerate(raws):
        who = me if i % 2 == 0 else 1 - me
        patients = raw_ref.shape[1]
        first = pl.multiple_of(who * half + offset, CHUNK)
        out_ref[:, pl.ds(first, patients)] = raw_ref[...] * scale_ref[:, :1]
        offset += patients * (i % 2)
    ran_ref[...] = jnp.zeros(ran_ref.shape, f32)


def per_device(tensor, feat_init, time_init):
    feat_dev, time_dev, rows_dev = tensor.shape
    rank = feat_init.shape[0]
    total_pat = rows_dev * lax.axis_size("pat")
    total_feat = feat_dev * lax.axis_size("feat")
    cells, half = feat_dev * time_dev, rows_dev // 2
    flat = tensor.reshape(cells, rows_dev)
    swap = [(0, 1), (1, 0)]

    def from_core(x):
        return lax.ppermute(x, "feat", swap)

    def from_tm(x):
        return lax.ppermute(x, "tm", swap)

    def from_pat(x, flip):
        return lax.ppermute(x, "pat", [(i, i ^ flip) for i in range(lax.axis_size("pat"))])

    def from_both(x, flip):
        count = 2 * lax.axis_size("pat")
        return lax.ppermute(x, ("pat", "tm"), [(i, i ^ (2 * flip + 1)) for i in range(count)])

    square = ((rank, rank), f32)

    def load(patients):
        return dict(flops=patients, moved=patients)

    def long(patients):
        return dict(flops=10 * 6 * rank * cells * patients, moved=40 * cells * patients)

    def step(mine, offset, after, *operands, before=0, more=()):
        loads = [pltpu.SemaphoreType.DMA((LOADS,))] if after else []
        outs = [((rank, before), f32)] * (before > 0) + [((cells, after), f32)] * (after > 0) + list(more)
        specs = [VMEM] * (len(operands) - (after > 0)) + [HBM] * (after > 0)
        return call(lambda *refs: bring(half, mine, offset, *refs), outs, "bring", specs, loads, ROOM, **load(before))(*operands)

    time_rows = time_init.T
    c0, c1 = SHARES
    (kept_o0,) = step(False, 0, c0, flat)
    away_0, kept_m0, hl, time_rows = step(
        True, 0, c0, feat_init, time_rows, kept_o0, flat, before=c0, more=[((2 * rank, cells), bf16), ((rank, LANES), f32)]
    )
    arrived_0, feat_core = lax.optimization_barrier((from_core(away_0), from_core(feat_init)))
    own_0, kept_o1 = step(False, c0, c1, hl, kept_m0, flat, before=c0)
    mine = [own_0 + arrived_0]
    theirs = [from_tm(jnp.concatenate([mine[0], time_rows], axis=1))]
    away_1, kept_m1 = step(True, c0, c1, hl, kept_o1, flat, before=c1)
    arrived_1 = from_core(away_1)
    (own_1,) = step(None, 0, 0, hl, kept_m1, before=c1)
    mine.append(own_1 + arrived_1)
    theirs.append(from_tm(mine[1]))
    kept = [(kept_m0, kept_o0), (kept_m1, kept_o1)]

    packed = ((8, LANES), f32)
    payload = ((rank + 8, cells // 4), f32)
    summed = [((rank, cells), f32), square]
    few = dict(flops=2**20, moved=2**18)
    sofar, totals = (), []
    for count, patients in enumerate(SHARES):
        (total,) = call(add_piece, [((rank, patients), f32)], "add_piece", [VMEM] * 3, **few)(
            mine[count], theirs[count], *(sofar[1:] or [mine[-1]])
        )
        other = from_core(total)
        totals += [total, other]
        sofar = call(lambda *refs: weigh([0], *refs), summed, "weigh", [VMEM] * (2 + len(sofar)), **long(patients))(
            total, kept[count][0], *sofar
        )
        if count < len(SHARES) - 1:
            sofar = call(lambda *refs: weigh([0], *refs), summed, "weigh", [VMEM] * 4, **long(patients))(
                other, kept[count][1], *sofar
            )
    quarters = call(
        lambda *refs: weigh_last([0], *refs), [payload] * 4, "weigh_last", [VMEM] * 4,
        [pltpu.VMEM((rank, cells), f32), pltpu.VMEM((rank, rank), f32)], **long(patients)
    )(totals[-1], kept[-1][1], *sofar)
    inverse, time_gram = call(start_system, [square] * 2, "start_system", [VMEM] * 4, **few)(
        feat_init, feat_core, time_rows, theirs[0]
    )

    def over_ring(mine, third, second, first, shape, *after):
        (a,) = call(pair, [shape], "pair", [VMEM] * (2 + len(after)), **few)(mine, first, *after)
        (b,) = call(hold, [shape], "hold", [VMEM] * 2, **few)(second, a)
        return a, b, third

    a, b, c = over_ring(quarters[0], *[from_pat(quarters[i], i) for i in (1, 3, 2)], payload, inverse)
    part = a + (b + c)
    raws = [((rank, x.shape[1]), f32) for x in totals]
    *raws, solved = call(solve_pat, raws + [packed], "solve_pat", [VMEM] * (1 + len(totals)), **few)(inverse, *totals)
    a, b, c = over_ring(part, *[from_pat(part, flip) for flip in (8, 24, 16)], payload, solved)
    part, tail = call(add_and_project, [payload, packed], "add_and_project", [VMEM] * 5, **few)(a, b, c, time_rows, inverse)
    far, high, tm = from_both(part, 4), from_pat(part, 4), from_tm(tail)
    pat_gram, scale, solver = call(
        lambda *refs: feat_system(total_pat, *refs), [square, ((rank, LANES), f32), square], "feat_system", [VMEM] * 3, **few
    )(part, far, time_gram)
    (weighted,) = call(scale_weighted, [((rank, cells // 4), f32)], "scale_weighted", [VMEM] * 4, **few)(
        part, high, scale, solver
    )
    double = ((rank, 2 * LANES), f32)
    (sums,) = call(solve_feat, [double], "solve_feat", [VMEM] * 6, **few)(part, far, high, tm, weighted, solver)
    factor_pat, ran = call(scale_pat, [((rank, rows_dev), f32), packed], "scale_pat", [VMEM] * (1 + len(raws)), **few)(
        scale, *raws
    )
    a, b, c = over_ring(sums, *[from_pat(sums, flip) for flip in (1, 3, 2)], double, ran)
    total = a + (b + c)
    sums, feat_raw = total[:, :LANES], total[:, LANES:]
    factor_feat, factor_time = call(
        lambda *refs: solve_time(total_pat, total_feat, *refs),
        [((rank, feat_dev), f32), ((time_dev, rank), f32)],
        "solve_time", [VMEM] * 4, **few,
    )(sums, from_core(sums), feat_raw, pat_gram)
    return (factor_pat, factor_feat, factor_time.T)


def solution(mesh):
    placed = (P("feat", "tm", "pat"), P(None, "feat"), P(None, "tm"))
    return jax.shard_map(
        per_device,
        mesh=mesh,
        in_specs=placed,
        out_specs=(P(None, "pat"), P(None, "feat"), P(None, "tm")),
        check_vma=False,
    )
```

```python
import math

import jax
import jax.numpy as jnp
from jax import lax
from jax.experimental import pallas as pl
from jax.experimental.pallas import tpu as pltpu
from jax.sharding import PartitionSpec as P

f32, bf16 = jnp.float32, jnp.bfloat16
highest = lax.Precision.HIGHEST
epsilon = 1e-06
VMEM = pl.BlockSpec(memory_space=pltpu.VMEM)
HBM = pl.BlockSpec(memory_space=pltpu.HBM)
NN = (((1,), (0,)), ((), ()))
NT = (((1,), (1,)), ((), ()))
TN = (((0,), (0,)), ((), ()))
LANES = 128


def exact(a, b, dims=NN):
    return lax.dot_general(a, b, dims, precision=highest, preferred_element_type=f32)


def quick(a, b, dims=NN):
    return lax.dot_general(a, b, dims, preferred_element_type=f32)


def split(x):
    hi = x.astype(bf16)
    return hi, (x - hi.astype(f32)).astype(bf16)


def iota(shape, dim):
    return lax.broadcasted_iota(jnp.int32, shape, dim)


def one_hot_feat(feat, time):
    shape = (feat, feat * time)
    return jnp.where(lax.div(iota(shape, 1), time) == iota(shape, 0), 1.0, 0.0).astype(f32)


def one_hot_time(feat, time):
    shape = (time, feat * time)
    return jnp.where(lax.rem(iota(shape, 1), time) == iota(shape, 0), 1.0, 0.0).astype(f32)


def eliminate(tiles, group=16):
    rank = tiles[0].shape[0]
    rows = iota((rank, LANES), 0)
    for start in range(0, rank, group):
        columns = [
            jnp.broadcast_to(tiles[0][:, start + t : start + t + 1], (rank, LANES)) for t in range(group)
        ]
        for t in range(group):
            at = start + t
            column = columns[t]
            inverse = 1.0 / column[at : at + 1, :]
            here = rows == at
            for later in range(t + 1, group):
                scaled = columns[later][at : at + 1, :] * inverse
                columns[later] = jnp.where(here, scaled, columns[later] - column * scaled)
            new = []
            for tile in tiles:
                scaled = tile[at : at + 1, :] * inverse
                new.append(jnp.where(here, scaled, tile - column * scaled))
            tiles = new
    return tiles


def invert(system):
    rank = system.shape[0]
    eye = jnp.where(iota((rank, rank), 0) == iota((rank, rank), 1), 1.0, 0.0).astype(f32)
    (solved,) = eliminate([wide(jnp.concatenate([system, eye], axis=1))])
    return solved[:, rank : 2 * rank]


def wide(x, columns=LANES):
    return jnp.concatenate([x, jnp.zeros((x.shape[0], columns - x.shape[1]), f32)], axis=1)


def call(body, out_shape, name, specs, scratch=(), limit=24, flops=0, moved=0):
    return pl.pallas_call(
        body,
        out_shape=[jax.ShapeDtypeStruct(s, d) for s, d in out_shape],
        in_specs=specs,
        out_specs=[VMEM] * len(out_shape),
        scratch_shapes=list(scratch),
        compiler_params=pltpu.CompilerParams(vmem_limit_bytes=limit * 2**20),
        cost_estimate=pl.CostEstimate(flops=flops, bytes_accessed=moved, transcendentals=0),
        name=name,
    )


CHUNK = 256
SHARES = (1024, 1024)
LOADS = 4
ROOM = 40


def bring(half, mine, offset, *refs):
    refs = list(refs)
    sems = refs.pop() if mine is not None else None
    copies = []
    if mine is not None:
        build, there = {2: (False, False), 5: (False, True), 8: (True, True)}[len(refs)]
    else:
        build, there = False, True
    source = refs[: 2 * build + (there and not build)]
    refs = refs[len(source) :]
    there_ref = refs.pop(0) if there else None
    if mine is not None:
        block_ref, refs = refs[0], refs[1:]
        kept_ref = refs.pop(1 if there else 0)
        me = lax.axis_index("feat")
        first = pl.multiple_of((me if mine else 1 - me) * half + offset, CHUNK)
        cells, patients = kept_ref.shape
        step = cells // LOADS
        for i in range(LOADS):
            rows = pl.ds(i * step, step)
            copies.append(
                pltpu.make_async_copy(block_ref.at[rows, pl.ds(first, patients)], kept_ref.at[rows, :], sems.at[i])
            )
        for copy in copies:
            copy.start()
    if there:
        terms_ref = refs[0]
        rank, patients = terms_ref.shape
        if build:
            feat, time = source[0][...], source[1][...]
            hl_ref, time_ref = refs[1:]
            count = (feat.shape[1], time.shape[0])
            product = exact(feat, one_hot_feat(*count)) * exact(time, one_hot_time(*count), TN)
            hl_ref[...] = jnp.concatenate(split(product), axis=0)
            below = jnp.zeros((rank - time.shape[0], LANES), f32)
            time_ref[...] = jnp.concatenate([wide(time), below], axis=0)
        else:
            hl_ref = source[0]

        def contract(columns):
            total = None
            for d in range(0, there_ref.shape[0], CHUNK):
                hi, lo = split(there_ref[d : d + CHUNK, columns])
                both = quick(hl_ref[:, d : d + CHUNK], hi)
                part = both[:rank] + both[rank:] + quick(hl_ref[:rank, d : d + CHUNK], lo)
                total = part if total is None else total + part
            terms_ref[:, columns] = total

        if copies:
            @pl.loop(0, patients // CHUNK)
            def _(c):
                contract(pl.ds(pl.multiple_of(c * CHUNK, CHUNK), CHUNK))

        else:
            for c in range(0, patients, CHUNK):
                contract(slice(c, c + CHUNK))
    for copy in copies:
        copy.wait()


def bring_both(half, offset, hl_ref, before_ref, block_ref, terms_ref, other_ref, mine_ref, sems):
    me = lax.axis_index("feat")
    rank = terms_ref.shape[0]
    cells, patients = other_ref.shape
    step = cells // LOADS
    copies = []
    for part, (who, kept_ref) in enumerate(((1 - me, other_ref), (me, mine_ref))):
        first = pl.multiple_of(who * half + offset, CHUNK)
        for i in range(LOADS):
            rows = pl.ds(i * step, step)
            copies.append(
                pltpu.make_async_copy(
                    block_ref.at[rows, pl.ds(first, patients)], kept_ref.at[rows, :], sems.at[part * LOADS + i]
                )
            )
    for copy in copies:
        copy.start()
    for i in range(LOADS):
        copies[i].wait()
        rows = slice(i * step, (i + 1) * step)
        for c in range(0, patients, CHUNK):
            hi, lo = split(other_ref[rows, c : c + CHUNK])
            both = quick(hl_ref[:, rows], hi)
            part = both[:rank] + both[rank:] + quick(hl_ref[:rank, rows], lo)
            if i > 0:
                part = part + terms_ref[:, c : c + CHUNK]
            terms_ref[:, c : c + CHUNK] = part
    for copy in copies[LOADS:]:
        copy.wait()


def start_system(feat_ref, core_ref, time_ref, piece_ref, inverse_ref, time_gram_ref):
    rank = inverse_ref.shape[0]
    feat, feat_other = feat_ref[...], core_ref[...]
    time, time_other = time_ref[...], piece_ref[:, piece_ref.shape[1] - LANES :]
    time_gram = (exact(time, time, TN) + exact(time_other, time_other, TN))[:rank, :rank]
    system = (exact(feat, feat, NT) + exact(feat_other, feat_other, NT)) * time_gram
    inverse_ref[...] = invert(system)
    time_gram_ref[...] = time_gram


def solve_pat(inverse_ref, *refs):
    count = len(refs) // 2
    for terms_ref, out_ref in zip(refs[:count], refs[count:]):
        out_ref[...] = exact(inverse_ref[...], terms_ref[...])
    refs[-1][...] = jnp.zeros(refs[-1].shape, f32)


def add_piece(mine_ref, theirs_ref, *refs):
    out_ref = refs[-1]
    out_ref[...] = mine_ref[...] + theirs_ref[:, : mine_ref.shape[1]]


def pack(square):
    return jnp.concatenate([square[i : i + 8, :] for i in range(0, 32, 8)], axis=1)


def unpack(packed):
    return jnp.concatenate([packed[:, i : i + 32] for i in range(0, 128, 32)], axis=0)


def weigh(columns, *refs):
    pairs, (*before, out_ref, gram_ref) = refs[: 2 * len(columns)], refs[2 * len(columns) :]
    rank = gram_ref.shape[0]
    total = gram = None
    for i, first in enumerate(columns):
        terms_ref, kept_ref = pairs[2 * i : 2 * i + 2]
        hi, lo = split(terms_ref[...])
        hl = jnp.concatenate([hi, lo], axis=0)
        for c in range(0, terms_ref.shape[1], CHUNK):
            kept_hi, kept_lo = split(kept_ref[:, first + c : first + c + CHUNK])
            both = quick(kept_hi, hl[:, c : c + CHUNK], NT)
            part = both[:, :rank] + both[:, rank:] + quick(kept_lo, hl[:rank, c : c + CHUNK], NT)
            total = part if total is None else total + part
        square = exact(terms_ref[...], terms_ref[...], NT)
        gram = square if gram is None else gram + square
    weighted = total.T
    if before:
        weighted, gram = weighted + before[0][...], gram + before[1][...]
    out_ref[...] = weighted
    gram_ref[...] = gram


def weigh_last(columns, *refs):
    *ins, q0, q1, q2, q3, total_ref, gram_ref = refs
    weigh(columns, *ins, total_ref, gram_ref)
    rank, cells = q0.shape[0] - 8, q0.shape[1]
    gram = wide(pack(gram_ref[...]), cells)
    me = lax.rem(lax.axis_index("pat"), 4)
    for flip, out_ref in enumerate((q0, q1, q2, q3)):
        first = pl.multiple_of(lax.bitwise_xor(me, flip) * cells, cells)
        out_ref[:rank, :] = total_ref[:, pl.ds(first, cells)]
        out_ref[rank:, :] = gram


def pair(a_ref, b_ref, *refs):
    refs[-1][...] = a_ref[...] + b_ref[...]


def hold(a_ref, first_ref, out_ref):
    out_ref[...] = a_ref[...]


def add_and_project(a_ref, b_ref, c_ref, time_ref, inverse_ref, out_ref, tail_ref):
    total = a_ref[...] + (b_ref[...] + c_ref[...])
    cells = total.shape[1]
    rank, feat_count = inverse_ref.shape[0], 32
    inverse = inverse_ref[...]
    weighted = exact(inverse, total[:rank, :])
    gram = pack(exact(exact(inverse, unpack(total[rank:, :LANES])), inverse, NT))
    time_count = cells // feat_count
    time = time_ref[:time_count, :rank]
    spread = exact(time, one_hot_time(feat_count, time_count), TN)
    terms = pack(exact(weighted * spread, one_hot_feat(feat_count, time_count), NT))
    out_ref[:rank, :] = weighted
    out_ref[rank:, :] = jnp.concatenate([gram, terms], axis=1)
    tail_ref[...] = terms


def diagonal(square):
    kept = jnp.where(iota(square.shape, 0) == iota(square.shape, 1), square, 0.0)
    return jnp.sum(kept, axis=1, keepdims=True), jnp.sum(kept, axis=0, keepdims=True)


def norms(square):
    column, row = diagonal(square)
    return 1.0 / jnp.sqrt(column + epsilon), 1.0 / jnp.sqrt(row + epsilon)


def feat_system(total_pat, own_ref, far_ref, time_gram_ref, gram_ref, scale_ref, solver_ref):
    rank = gram_ref.shape[0]
    gram = unpack(own_ref[rank:, :LANES] + far_ref[rank:, :LANES]) / total_pat
    column, row = norms(gram)
    pat_gram = gram * column * row
    gram_ref[...] = pat_gram
    scale_ref[...] = jnp.broadcast_to(column, scale_ref.shape)
    solver_ref[...] = invert(pat_gram * time_gram_ref[...]) * row


def scale_weighted(own_ref, high_ref, scale_ref, solver_ref, out_ref):
    rank = out_ref.shape[0]
    out_ref[...] = (own_ref[:rank, :] + high_ref[:rank, :]) * scale_ref[:, :1]


def solve_feat(own_ref, far_ref, high_ref, tm_ref, weighted_ref, solver_ref, out_ref):
    rank, cells = weighted_ref.shape
    feat_count = 32
    time_count = cells // feat_count
    terms = (own_ref[rank:, LANES:] + tm_ref[...]) + (high_ref[rank:, LANES:] + far_ref[rank:, LANES:])
    raw = exact(solver_ref[...], unpack(terms))
    spread = exact(raw, one_hot_feat(feat_count, time_count))
    time_terms = exact(weighted_ref[...] * spread, one_hot_time(feat_count, time_count), NT)
    out_ref[:, :LANES] = wide(jnp.concatenate([exact(raw, raw, NT), time_terms], axis=1))
    here = lax.div(iota((rank, LANES), 1), feat_count) == lax.rem(lax.axis_index("pat"), 4)
    out_ref[:, LANES:] = jnp.where(here, jnp.concatenate([raw] * 4, axis=1), 0.0)


def solve_time(total_pat, total_feat, a_ref, b_ref, raw_ref, gram_ref, feat_ref, time_ref):
    time_count, rank = time_ref.shape
    total = a_ref[...] + b_ref[...]
    gram = total[:, :rank] / total_feat
    column, row = norms(gram)
    feat_ref[...] = raw_ref[...] * column
    system = gram_ref[...] * (gram * column * row)
    terms = total[:, rank : rank + time_count] * column
    (solved,) = eliminate([wide(jnp.concatenate([system, terms], axis=1))])
    place = jnp.where(iota((time_count, LANES), 1) == iota((time_count, LANES), 0) + rank, 1.0, 0.0).astype(f32)
    factor = exact(place, solved, NT)
    time_ref[...] = factor * (1.0 / math.sqrt(total_pat * total_feat))


def scale_pat(scale_ref, *refs):
    *raws, out_ref, ran_ref = refs
    me = lax.axis_index("feat")
    half = out_ref.shape[1] // 2
    offset = 0
    for i, raw_ref in enumerate(raws):
        who = me if i % 2 == 0 else 1 - me
        patients = raw_ref.shape[1]
        first = pl.multiple_of(who * half + offset, CHUNK)
        out_ref[:, pl.ds(first, patients)] = raw_ref[...] * scale_ref[:, :1]
        offset += patients * (i % 2)
    ran_ref[...] = jnp.zeros(ran_ref.shape, f32)


def per_device(tensor, feat_init, time_init):
    feat_dev, time_dev, rows_dev = tensor.shape
    rank = feat_init.shape[0]
    total_pat = rows_dev * lax.axis_size("pat")
    total_feat = feat_dev * lax.axis_size("feat")
    cells, half = feat_dev * time_dev, rows_dev // 2
    flat = tensor.reshape(cells, rows_dev)
    swap = [(0, 1), (1, 0)]

    def from_core(x):
        return lax.ppermute(x, "feat", swap)

    def from_tm(x):
        return lax.ppermute(x, "tm", swap)

    def from_pat(x, flip):
        return lax.ppermute(x, "pat", [(i, i ^ flip) for i in range(lax.axis_size("pat"))])

    def from_both(x, flip):
        count = 2 * lax.axis_size("pat")
        return lax.ppermute(x, ("pat", "tm"), [(i, i ^ (2 * flip + 1)) for i in range(count)])

    square = ((rank, rank), f32)

    def load(patients):
        return dict(flops=patients, moved=patients)

    def long(patients):
        return dict(flops=10 * 6 * rank * cells * patients, moved=40 * cells * patients)

    def step(mine, offset, after, *operands, before=0, more=()):
        loads = [pltpu.SemaphoreType.DMA((LOADS,))] if after else []
        outs = [((rank, before), f32)] * (before > 0) + [((cells, after), f32)] * (after > 0) + list(more)
        specs = [VMEM] * (len(operands) - (after > 0)) + [HBM] * (after > 0)
        return call(lambda *refs: bring(half, mine, offset, *refs), outs, "bring", specs, loads, ROOM, **load(before))(*operands)

    time_rows = time_init.T
    c0, c1 = SHARES
    (kept_o0,) = step(False, 0, c0, flat)
    away_0, kept_m0, hl, time_rows = step(
        True, 0, c0, feat_init, time_rows, kept_o0, flat, before=c0, more=[((2 * rank, cells), bf16), ((rank, LANES), f32)]
    )
    arrived_0, feat_core = lax.optimization_barrier((from_core(away_0), from_core(feat_init)))
    (own_0,) = step(None, 0, 0, hl, kept_m0, before=c0)
    mine = [own_0 + arrived_0]
    theirs = [from_tm(jnp.concatenate([mine[0], time_rows], axis=1))]
    away_1, kept_o1, kept_m1 = call(
        lambda *refs: bring_both(half, c0, *refs), [((rank, c1), f32), ((cells, c1), f32), ((cells, c1), f32)],
        "bring_both", [VMEM, VMEM, HBM], [pltpu.SemaphoreType.DMA((2 * LOADS,))], ROOM, **load(c1),
    )(hl, own_0, flat)
    arrived_1 = from_core(away_1)
    (own_1,) = step(None, 0, 0, hl, kept_m1, before=c1)
    mine.append(own_1 + arrived_1)
    theirs.append(from_tm(mine[1]))
    kept = [(kept_m0, kept_o0), (kept_m1, kept_o1)]

    packed = ((8, LANES), f32)
    payload = ((rank + 8, cells // 4), f32)
    summed = [((rank, cells), f32), square]
    few = dict(flops=2**20, moved=2**18)
    sofar, totals = (), []
    for count, patients in enumerate(SHARES):
        (total,) = call(add_piece, [((rank, patients), f32)], "add_piece", [VMEM] * 3, **few)(
            mine[count], theirs[count], *(sofar[1:] or [mine[-1]])
        )
        other = from_core(total)
        totals += [total, other]
        sofar = call(lambda *refs: weigh([0], *refs), summed, "weigh", [VMEM] * (2 + len(sofar)), **long(patients))(
            total, kept[count][0], *sofar
        )
        if count < len(SHARES) - 1:
            sofar = call(lambda *refs: weigh([0], *refs), summed, "weigh", [VMEM] * 4, **long(patients))(
                other, kept[count][1], *sofar
            )
    quarters = call(
        lambda *refs: weigh_last([0], *refs), [payload] * 4, "weigh_last", [VMEM] * 4,
        [pltpu.VMEM((rank, cells), f32), pltpu.VMEM((rank, rank), f32)], **long(patients)
    )(totals[-1], kept[-1][1], *sofar)
    inverse, time_gram = call(start_system, [square] * 2, "start_system", [VMEM] * 4, **few)(
        feat_init, feat_core, time_rows, theirs[0]
    )

    def over_ring(mine, third, second, first, shape, *after):
        (a,) = call(pair, [shape], "pair", [VMEM] * (2 + len(after)), **few)(mine, first, *after)
        (b,) = call(hold, [shape], "hold", [VMEM] * 2, **few)(second, a)
        return a, b, third

    a, b, c = over_ring(quarters[0], *[from_pat(quarters[i], i) for i in (1, 3, 2)], payload, inverse)
    part = a + (b + c)
    raws = [((rank, x.shape[1]), f32) for x in totals]
    *raws, solved = call(solve_pat, raws + [packed], "solve_pat", [VMEM] * (1 + len(totals)), **few)(inverse, *totals)
    a, b, c = over_ring(part, *[from_pat(part, flip) for flip in (8, 24, 16)], payload, solved)
    part, tail = call(add_and_project, [payload, packed], "add_and_project", [VMEM] * 5, **few)(a, b, c, time_rows, inverse)
    far, high, tm = from_both(part, 4), from_pat(part, 4), from_tm(tail)
    pat_gram, scale, solver = call(
        lambda *refs: feat_system(total_pat, *refs), [square, ((rank, LANES), f32), square], "feat_system", [VMEM] * 3, **few
    )(part, far, time_gram)
    (weighted,) = call(scale_weighted, [((rank, cells // 4), f32)], "scale_weighted", [VMEM] * 4, **few)(
        part, high, scale, solver
    )
    double = ((rank, 2 * LANES), f32)
    (sums,) = call(solve_feat, [double], "solve_feat", [VMEM] * 6, **few)(part, far, high, tm, weighted, solver)
    factor_pat, ran = call(scale_pat, [((rank, rows_dev), f32), packed], "scale_pat", [VMEM] * (1 + len(raws)), **few)(
        scale, *raws
    )
    a, b, c = over_ring(sums, *[from_pat(sums, flip) for flip in (1, 3, 2)], double, ran)
    total = a + (b + c)
    sums, feat_raw = total[:, :LANES], total[:, LANES:]
    factor_feat, factor_time = call(
        lambda *refs: solve_time(total_pat, total_feat, *refs),
        [((rank, feat_dev), f32), ((time_dev, rank), f32)],
        "solve_time", [VMEM] * 4, **few,
    )(sums, from_core(sums), feat_raw, pat_gram)
    return (factor_pat, factor_feat, factor_time.T)


def solution(mesh):
    placed = (P("feat", "tm", "pat"), P(None, "feat"), P(None, "tm"))
    return jax.shard_map(
        per_device,
        mesh=mesh,
        in_specs=placed,
        out_specs=(P(None, "pat"), P(None, "feat"), P(None, "tm")),
        check_vma=False,
    )
```

```python
import math

import jax
import jax.numpy as jnp
from jax import lax
from jax.experimental import pallas as pl
from jax.experimental.pallas import tpu as pltpu
from jax.sharding import PartitionSpec as P

f32, bf16 = jnp.float32, jnp.bfloat16
highest = lax.Precision.HIGHEST
epsilon = 1e-06
VMEM = pl.BlockSpec(memory_space=pltpu.VMEM)
HBM = pl.BlockSpec(memory_space=pltpu.HBM)
NN = (((1,), (0,)), ((), ()))
NT = (((1,), (1,)), ((), ()))
TN = (((0,), (0,)), ((), ()))
LANES = 128


def exact(a, b, dims=NN):
    return lax.dot_general(a, b, dims, precision=highest, preferred_element_type=f32)


def quick(a, b, dims=NN):
    return lax.dot_general(a, b, dims, preferred_element_type=f32)


def split(x):
    hi = x.astype(bf16)
    return hi, (x - hi.astype(f32)).astype(bf16)


def iota(shape, dim):
    return lax.broadcasted_iota(jnp.int32, shape, dim)


def one_hot_feat(feat, time):
    shape = (feat, feat * time)
    return jnp.where(lax.div(iota(shape, 1), time) == iota(shape, 0), 1.0, 0.0).astype(f32)


def one_hot_time(feat, time):
    shape = (time, feat * time)
    return jnp.where(lax.rem(iota(shape, 1), time) == iota(shape, 0), 1.0, 0.0).astype(f32)


def eliminate(tiles, group=16):
    rank = tiles[0].shape[0]
    rows = iota((rank, LANES), 0)
    for start in range(0, rank, group):
        columns = [
            jnp.broadcast_to(tiles[0][:, start + t : start + t + 1], (rank, LANES)) for t in range(group)
        ]
        for t in range(group):
            at = start + t
            column = columns[t]
            inverse = 1.0 / column[at : at + 1, :]
            here = rows == at
            for later in range(t + 1, group):
                scaled = columns[later][at : at + 1, :] * inverse
                columns[later] = jnp.where(here, scaled, columns[later] - column * scaled)
            new = []
            for tile in tiles:
                scaled = tile[at : at + 1, :] * inverse
                new.append(jnp.where(here, scaled, tile - column * scaled))
            tiles = new
    return tiles


def invert(system):
    rank = system.shape[0]
    eye = jnp.where(iota((rank, rank), 0) == iota((rank, rank), 1), 1.0, 0.0).astype(f32)
    (solved,) = eliminate([wide(jnp.concatenate([system, eye], axis=1))])
    return solved[:, rank : 2 * rank]


def wide(x, columns=LANES):
    return jnp.concatenate([x, jnp.zeros((x.shape[0], columns - x.shape[1]), f32)], axis=1)


def call(body, out_shape, name, specs, scratch=(), limit=24, flops=0, moved=0):
    return pl.pallas_call(
        body,
        out_shape=[jax.ShapeDtypeStruct(s, d) for s, d in out_shape],
        in_specs=specs,
        out_specs=[VMEM] * len(out_shape),
        scratch_shapes=list(scratch),
        compiler_params=pltpu.CompilerParams(vmem_limit_bytes=limit * 2**20),
        cost_estimate=pl.CostEstimate(flops=flops, bytes_accessed=moved, transcendentals=0),
        name=name,
    )


CHUNK = 256
SHARES = (1024, 1024)
LOADS = 4
ROOM = 40


def contract(hl_ref, there_ref, terms_ref):
    rank, patients = terms_ref.shape
    for c in range(0, patients, CHUNK):
        total = None
        for d in range(0, there_ref.shape[0], CHUNK):
            hi, lo = split(there_ref[d : d + CHUNK, c : c + CHUNK])
            both = quick(hl_ref[:, d : d + CHUNK], hi)
            part = both[:rank] + both[rank:] + quick(hl_ref[:rank, d : d + CHUNK], lo)
            total = part if total is None else total + part
        terms_ref[:, c : c + CHUNK] = total


def bring_both(half, offset, hl_ref, before_ref, block_ref, terms_ref, other_ref, mine_ref, sems, build=None):
    me = lax.axis_index("feat")
    rank = terms_ref.shape[0]
    cells, patients = other_ref.shape
    step = cells // LOADS
    copies = []
    for part, (who, kept_ref) in enumerate(((1 - me, other_ref), (me, mine_ref))):
        first = pl.multiple_of(who * half + offset, CHUNK)
        for i in range(LOADS):
            rows = pl.ds(i * step, step)
            copies.append(
                pltpu.make_async_copy(
                    block_ref.at[rows, pl.ds(first, patients)], kept_ref.at[rows, :], sems.at[part * LOADS + i]
                )
            )
    for copy in copies:
        copy.start()
    if build is not None:
        build()
    for i in range(LOADS):
        copies[i].wait()
        rows = slice(i * step, (i + 1) * step)
        for c in range(0, patients, CHUNK):
            hi, lo = split(other_ref[rows, c : c + CHUNK])
            both = quick(hl_ref[:, rows], hi)
            part = both[:rank] + both[rank:] + quick(hl_ref[:rank, rows], lo)
            if i > 0:
                part = part + terms_ref[:, c : c + CHUNK]
            terms_ref[:, c : c + CHUNK] = part
    for copy in copies[LOADS:]:
        copy.wait()


def bring_first(half, init_ref, block_ref, terms_ref, other_ref, mine_ref, hl_ref, time_ref, sems):
    def build():
        rank = terms_ref.shape[0]
        feat, time = init_ref[:rank, :], init_ref[rank:, :rank]
        count = (feat.shape[1], time.shape[0])
        product = exact(feat, one_hot_feat(*count)) * exact(time, one_hot_time(*count), TN)
        hl_ref[...] = jnp.concatenate(split(product), axis=0)
        below = jnp.zeros((rank - time.shape[0], LANES), f32)
        time_ref[...] = jnp.concatenate([wide(time), below], axis=0)

    bring_both(half, 0, hl_ref, None, block_ref, terms_ref, other_ref, mine_ref, sems, build)


def start_system(feat_ref, core_ref, time_ref, piece_ref, inverse_ref, time_gram_ref):
    rank = inverse_ref.shape[0]
    feat, feat_other = feat_ref[:rank, :], core_ref[:rank, :]
    time, time_other = time_ref[...], piece_ref[:, piece_ref.shape[1] - LANES :]
    time_gram = (exact(time, time, TN) + exact(time_other, time_other, TN))[:rank, :rank]
    system = (exact(feat, feat, NT) + exact(feat_other, feat_other, NT)) * time_gram
    inverse_ref[...] = invert(system)
    time_gram_ref[...] = time_gram


def solve_pat(inverse_ref, *refs):
    count = len(refs) // 2
    for terms_ref, out_ref in zip(refs[:count], refs[count:]):
        out_ref[...] = exact(inverse_ref[...], terms_ref[...])
    refs[-1][...] = jnp.zeros(refs[-1].shape, f32)


def add_piece(mine_ref, theirs_ref, *refs):
    out_ref = refs[-1]
    out_ref[...] = mine_ref[...] + theirs_ref[:, : mine_ref.shape[1]]


def pack(square):
    return jnp.concatenate([square[i : i + 8, :] for i in range(0, 32, 8)], axis=1)


def unpack(packed):
    return jnp.concatenate([packed[:, i : i + 32] for i in range(0, 128, 32)], axis=0)


def weigh(columns, *refs):
    pairs, (*before, out_ref, gram_ref) = refs[: 2 * len(columns)], refs[2 * len(columns) :]
    rank = gram_ref.shape[0]
    total = gram = None
    for i, first in enumerate(columns):
        terms_ref, kept_ref = pairs[2 * i : 2 * i + 2]
        hi, lo = split(terms_ref[...])
        hl = jnp.concatenate([hi, lo], axis=0)
        for c in range(0, terms_ref.shape[1], CHUNK):
            kept_hi, kept_lo = split(kept_ref[:, first + c : first + c + CHUNK])
            both = quick(kept_hi, hl[:, c : c + CHUNK], NT)
            part = both[:, :rank] + both[:, rank:] + quick(kept_lo, hl[:rank, c : c + CHUNK], NT)
            total = part if total is None else total + part
        square = exact(terms_ref[...], terms_ref[...], NT)
        gram = square if gram is None else gram + square
    weighted = total.T
    if before:
        weighted, gram = weighted + before[0][...], gram + before[1][...]
    out_ref[...] = weighted
    gram_ref[...] = gram


def weigh_last(columns, *refs):
    *ins, q0, q1, q2, q3, total_ref, gram_ref = refs
    weigh(columns, *ins, total_ref, gram_ref)
    rank, cells = q0.shape[0] - 8, q0.shape[1]
    gram = wide(pack(gram_ref[...]), cells)
    me = lax.rem(lax.axis_index("pat"), 4)
    for flip, out_ref in enumerate((q0, q1, q2, q3)):
        first = pl.multiple_of(lax.bitwise_xor(me, flip) * cells, cells)
        out_ref[:rank, :] = total_ref[:, pl.ds(first, cells)]
        out_ref[rank:, :] = gram


def pair(a_ref, b_ref, *refs):
    refs[-1][...] = a_ref[...] + b_ref[...]


def hold(a_ref, first_ref, out_ref):
    out_ref[...] = a_ref[...]


def add_and_project(a_ref, b_ref, c_ref, time_ref, inverse_ref, out_ref, tail_ref):
    total = a_ref[...] + (b_ref[...] + c_ref[...])
    cells = total.shape[1]
    rank, feat_count = inverse_ref.shape[0], 32
    inverse = inverse_ref[...]
    weighted = exact(inverse, total[:rank, :])
    gram = pack(exact(exact(inverse, unpack(total[rank:, :LANES])), inverse, NT))
    time_count = cells // feat_count
    time = time_ref[:time_count, :rank]
    spread = exact(time, one_hot_time(feat_count, time_count), TN)
    terms = pack(exact(weighted * spread, one_hot_feat(feat_count, time_count), NT))
    out_ref[:rank, :] = weighted
    out_ref[rank:, :] = jnp.concatenate([gram, terms], axis=1)
    tail_ref[...] = terms


def diagonal(square):
    kept = jnp.where(iota(square.shape, 0) == iota(square.shape, 1), square, 0.0)
    return jnp.sum(kept, axis=1, keepdims=True), jnp.sum(kept, axis=0, keepdims=True)


def norms(square):
    column, row = diagonal(square)
    return 1.0 / jnp.sqrt(column + epsilon), 1.0 / jnp.sqrt(row + epsilon)


def feat_system(total_pat, own_ref, far_ref, time_gram_ref, gram_ref, scale_ref, solver_ref):
    rank = gram_ref.shape[0]
    gram = unpack(own_ref[rank:, :LANES] + far_ref[rank:, :LANES]) / total_pat
    column, row = norms(gram)
    pat_gram = gram * column * row
    gram_ref[...] = pat_gram
    scale_ref[...] = jnp.broadcast_to(column, scale_ref.shape)
    solver_ref[...] = invert(pat_gram * time_gram_ref[...]) * row


def scale_weighted(own_ref, high_ref, scale_ref, solver_ref, out_ref):
    rank = out_ref.shape[0]
    out_ref[...] = (own_ref[:rank, :] + high_ref[:rank, :]) * scale_ref[:, :1]


def solve_feat(own_ref, far_ref, high_ref, tm_ref, weighted_ref, solver_ref, out_ref):
    rank, cells = weighted_ref.shape
    feat_count = 32
    time_count = cells // feat_count
    terms = (own_ref[rank:, LANES:] + tm_ref[...]) + (high_ref[rank:, LANES:] + far_ref[rank:, LANES:])
    raw = exact(solver_ref[...], unpack(terms))
    spread = exact(raw, one_hot_feat(feat_count, time_count))
    time_terms = exact(weighted_ref[...] * spread, one_hot_time(feat_count, time_count), NT)
    out_ref[:, :LANES] = wide(jnp.concatenate([exact(raw, raw, NT), time_terms], axis=1))
    here = lax.div(iota((rank, LANES), 1), feat_count) == lax.rem(lax.axis_index("pat"), 4)
    out_ref[:, LANES:] = jnp.where(here, jnp.concatenate([raw] * 4, axis=1), 0.0)


def solve_time(total_pat, total_feat, a_ref, b_ref, raw_ref, gram_ref, feat_ref, time_ref):
    time_count, rank = time_ref.shape
    total = a_ref[...] + b_ref[...]
    gram = total[:, :rank] / total_feat
    column, row = norms(gram)
    feat_ref[...] = raw_ref[...] * column
    system = gram_ref[...] * (gram * column * row)
    terms = total[:, rank : rank + time_count] * column
    (solved,) = eliminate([wide(jnp.concatenate([system, terms], axis=1))])
    place = jnp.where(iota((time_count, LANES), 1) == iota((time_count, LANES), 0) + rank, 1.0, 0.0).astype(f32)
    factor = exact(place, solved, NT)
    time_ref[...] = factor * (1.0 / math.sqrt(total_pat * total_feat))


def scale_pat(scale_ref, *refs):
    *raws, out_ref, ran_ref = refs
    me = lax.axis_index("feat")
    half = out_ref.shape[1] // 2
    offset = 0
    for i, raw_ref in enumerate(raws):
        who = me if i % 2 == 0 else 1 - me
        patients = raw_ref.shape[1]
        first = pl.multiple_of(who * half + offset, CHUNK)
        out_ref[:, pl.ds(first, patients)] = raw_ref[...] * scale_ref[:, :1]
        offset += patients * (i % 2)
    ran_ref[...] = jnp.zeros(ran_ref.shape, f32)


def per_device(tensor, feat_init, time_init):
    feat_dev, time_dev, rows_dev = tensor.shape
    rank = feat_init.shape[0]
    total_pat = rows_dev * lax.axis_size("pat")
    total_feat = feat_dev * lax.axis_size("feat")
    cells, half = feat_dev * time_dev, rows_dev // 2
    flat = tensor.reshape(cells, rows_dev)
    swap = [(0, 1), (1, 0)]

    def from_core(x):
        return lax.ppermute(x, "feat", swap)

    def from_tm(x):
        return lax.ppermute(x, "tm", swap)

    def from_pat(x, flip):
        return lax.ppermute(x, "pat", [(i, i ^ flip) for i in range(lax.axis_size("pat"))])

    def from_both(x, flip):
        count = 2 * lax.axis_size("pat")
        return lax.ppermute(x, ("pat", "tm"), [(i, i ^ (2 * flip + 1)) for i in range(count)])

    square = ((rank, rank), f32)

    def load(patients):
        return dict(flops=patients, moved=patients)

    def long(patients):
        return dict(flops=10 * 6 * rank * cells * patients, moved=40 * cells * patients)

    def contracted(hl, there):
        patients = there.shape[1]
        return call(contract, [((rank, patients), f32)], "contract", [VMEM] * 2, **load(patients))(hl, there)[0]

    c0, c1 = SHARES
    both = [pltpu.SemaphoreType.DMA((2 * LOADS,))]
    init = jnp.concatenate([feat_init, jnp.pad(time_init.T, ((0, 0), (0, feat_dev - rank)))], axis=0)
    away_0, kept_o0, kept_m0, hl, time_rows = call(
        lambda *refs: bring_first(half, *refs),
        [((rank, c0), f32), ((cells, c0), f32), ((cells, c0), f32), ((2 * rank, cells), bf16), ((rank, LANES), f32)],
        "bring_first", [VMEM, HBM], both, ROOM, **load(c0),
    )(init, flat)
    arrived_0, init_core = lax.optimization_barrier((from_core(away_0), from_core(init)))
    own_0 = contracted(hl, kept_m0)
    mine = [own_0 + arrived_0]
    theirs = [from_tm(jnp.concatenate([mine[0], time_rows], axis=1))]
    away_1, kept_o1, kept_m1 = call(
        lambda *refs: bring_both(half, c0, *refs), [((rank, c1), f32), ((cells, c1), f32), ((cells, c1), f32)],
        "bring_both", [VMEM, VMEM, HBM], both, ROOM, **load(c1),
    )(hl, own_0, flat)
    arrived_1 = from_core(away_1)
    own_1 = contracted(hl, kept_m1)
    mine.append(own_1 + arrived_1)
    theirs.append(from_tm(mine[1]))
    kept = [(kept_m0, kept_o0), (kept_m1, kept_o1)]

    packed = ((8, LANES), f32)
    payload = ((rank + 8, cells // 4), f32)
    summed = [((rank, cells), f32), square]
    few = dict(flops=2**20, moved=2**18)
    sofar, totals = (), []
    for count, patients in enumerate(SHARES):
        (total,) = call(add_piece, [((rank, patients), f32)], "add_piece", [VMEM] * 3, **few)(
            mine[count], theirs[count], *(sofar[1:] or [mine[-1]])
        )
        other = from_core(total)
        totals += [total, other]
        sofar = call(lambda *refs: weigh([0], *refs), summed, "weigh", [VMEM] * (2 + len(sofar)), **long(patients))(
            total, kept[count][0], *sofar
        )
        if count < len(SHARES) - 1:
            sofar = call(lambda *refs: weigh([0], *refs), summed, "weigh", [VMEM] * 4, **long(patients))(
                other, kept[count][1], *sofar
            )
    quarters = call(
        lambda *refs: weigh_last([0], *refs), [payload] * 4, "weigh_last", [VMEM] * 4,
        [pltpu.VMEM((rank, cells), f32), pltpu.VMEM((rank, rank), f32)], **long(patients)
    )(totals[-1], kept[-1][1], *sofar)
    inverse, time_gram = call(start_system, [square] * 2, "start_system", [VMEM] * 4, **few)(
        init, init_core, time_rows, theirs[0]
    )

    def over_ring(mine, third, second, first, shape, *after):
        (a,) = call(pair, [shape], "pair", [VMEM] * (2 + len(after)), **few)(mine, first, *after)
        (b,) = call(hold, [shape], "hold", [VMEM] * 2, **few)(second, a)
        return a, b, third

    a, b, c = over_ring(quarters[0], *[from_pat(quarters[i], i) for i in (1, 3, 2)], payload, inverse)
    part = a + (b + c)
    raws = [((rank, x.shape[1]), f32) for x in totals]
    *raws, solved = call(solve_pat, raws + [packed], "solve_pat", [VMEM] * (1 + len(totals)), **few)(inverse, *totals)
    a, b, c = over_ring(part, *[from_pat(part, flip) for flip in (8, 24, 16)], payload, solved)
    part, tail = call(add_and_project, [payload, packed], "add_and_project", [VMEM] * 5, **few)(a, b, c, time_rows, inverse)
    far, high, tm = from_both(part, 4), from_pat(part, 4), from_tm(tail)
    pat_gram, scale, solver = call(
        lambda *refs: feat_system(total_pat, *refs), [square, ((rank, LANES), f32), square], "feat_system", [VMEM] * 3, **few
    )(part, far, time_gram)
    (weighted,) = call(scale_weighted, [((rank, cells // 4), f32)], "scale_weighted", [VMEM] * 4, **few)(
        part, high, scale, solver
    )
    double = ((rank, 2 * LANES), f32)
    (sums,) = call(solve_feat, [double], "solve_feat", [VMEM] * 6, **few)(part, far, high, tm, weighted, solver)
    factor_pat, ran = call(scale_pat, [((rank, rows_dev), f32), packed], "scale_pat", [VMEM] * (1 + len(raws)), **few)(
        scale, *raws
    )
    a, b, c = over_ring(sums, *[from_pat(sums, flip) for flip in (1, 3, 2)], double, ran)
    total = a + (b + c)
    sums, feat_raw = total[:, :LANES], total[:, LANES:]
    factor_feat, factor_time = call(
        lambda *refs: solve_time(total_pat, total_feat, *refs),
        [((rank, feat_dev), f32), ((time_dev, rank), f32)],
        "solve_time", [VMEM] * 4, **few,
    )(sums, from_core(sums), feat_raw, pat_gram)
    return (factor_pat, factor_feat, factor_time.T)


def solution(mesh):
    placed = (P("feat", "tm", "pat"), P(None, "feat"), P(None, "tm"))
    return jax.shard_map(
        per_device,
        mesh=mesh,
        in_specs=placed,
        out_specs=(P(None, "pat"), P(None, "feat"), P(None, "tm")),
        check_vma=False,
    )
```
